32 devices in a mesh: seq: 4 (over y, x), own: 8 (over z, core).
Axes of the slice: x: 2, y: 2, z: 4, core: 2. Of those that a mesh axis runs over, the one named last changes fastest.
Arguments:
- queries: bfloat16 [8, 512, 1024], P('own', 'seq'), may hold values from -6 to 6
- keys: bfloat16 [8, 512, 1024], P('own', 'seq'), may hold values from -6 to 6
- values: bfloat16 [8, 512, 1024], P('own', 'seq'), may hold values from -6 to 6
- gates: bfloat16 [8, 512, 1024], P('own', 'seq'), may hold values from -6 to 6
- lengths: int32 [8, 4], P('own'), may hold values from 1 to 256, 512 in all within a row
- gain: float32 [1024], replicated, may hold values from 0.1 to 1.9
- grad_out: bfloat16 [8, 512, 1024], P('own', 'seq'), may hold values from -6 to 6
Outputs:
- output: bfloat16 [8, 512, 1024], P('own', 'seq')
- grad_queries: bfloat16 [8, 512, 1024], P('own', 'seq')
- grad_keys: bfloat16 [8, 512, 1024], P('own', 'seq')
- grad_values: bfloat16 [8, 512, 1024], P('own', 'seq')
- grad_gates: bfloat16 [8, 512, 1024], P('own', 'seq')
- grad_gain: float32 [1024], replicated
The draws below stay inside these ranges and needn't reach their ends.
Inputs may be any that keep to these rules, and one draw needn't show every extreme that they name: Each group's 4 lengths sum to 512; in every group the longest is exactly 256.
All inputs are finite; a program needn't handle non-finite values.
Results may differ from the reference program's by a relative error of at most 0.0058.
Values may be sent and summed in bfloat16 or wider, within the bound.
A program may use at most 128 MiB of HBM per device.

```python
import math
import jax
import jax.numpy as jnp
import numpy as np
from jax import lax

D = 1024
H = 8
USERS = 4
SEQLEN = 512
MAXLEN = 256
GROUPS = 8


def level_of(own_key, dims, shards, low, largest):
    def one(dim, parts):
        draws = jax.random.uniform(jax.random.fold_in(jax.random.fold_in(own_key, 6), dim), (parts,), jnp.float32, low / len(shards), largest / len(shards))
        return jnp.repeat(jnp.exp(draws), dims[dim] // parts).reshape((-1,) + (1,) * (len(dims) - dim - 1))

    level = one(*shards[0])
    for cut in shards[1:]:
        level = level * one(*cut)
    return level


def length_profile(count, total, bound, lean):
    loads = [(1 << 20) // math.isqrt(rank ** lean) + 1 for rank in range(2, count + 1)]
    spare, counts = total - bound - (count - 1), [1] * (count - 1)
    while spare > 0:
        candidates = [i for i in range(count - 1) if counts[i] < bound]
        whole, left = sum([loads[i] for i in candidates]), spare
        for i in candidates:
            more = min(bound - counts[i], max(1, left * loads[i] // whole), spare)
            counts[i] = counts[i] + more
            spare = spare - more
    return np.array([bound] + counts)


def uneven_parts(key, number_of, total, most, lean):
    if number_of == 2:
        one = jax.random.randint(key, (), max(1, total - most), min(most, total - 1) + 1)
        return jnp.stack([one, total - one])
    sizes = jnp.asarray(length_profile(number_of, total, most, lean), jnp.int32)
    twos = (number_of - 1) // 2
    source_of, taker = sizes[1:1 + 2 * twos:2], sizes[2:2 + 2 * twos:2]
    slack = jnp.minimum(source_of - 1, most - taker)
    moved = jax.random.randint(jax.random.fold_in(key, 1), (twos,), 0, 1 << 20) % (slack + 1)
    sizes = sizes.at[1:1 + 2 * twos:2].set(source_of - moved).at[2:2 + 2 * twos:2].set(taker + moved)
    return sizes[jax.random.permutation(jax.random.fold_in(key, 2), number_of)]


def noise(key, extent, scale, limit, shards=(), kind=jnp.bfloat16):
    entries = jax.random.normal(key, extent, jnp.float32) * scale
    if len(shards) > 0:
        entries = level_of(key, extent, shards, -0.22, 0.18) * entries
    return jnp.clip(entries, min=-limit, max=limit).astype(kind)


def setup_inputs(seed: int = 0) -> dict:
    streams_of = jax.random.split(jax.random.key(seed), 8)
    queries = noise(streams_of[0], (GROUPS, SEQLEN, D), 1.0, 6.0, ((0, 8), (1, 4)))
    keys = noise(streams_of[1], (GROUPS, SEQLEN, D), 1.0, 6.0, ((0, 8), (1, 4)))
    values = noise(streams_of[2], (GROUPS, SEQLEN, D), 1.0, 6.0, ((0, 8), (1, 4)))
    gates = noise(streams_of[3], (GROUPS, SEQLEN, D), 1.0, 6.0, ((0, 8), (1, 4)))
    lengths = jax.vmap(lambda own: uneven_parts(own, USERS, SEQLEN, MAXLEN, 2))(jax.random.split(streams_of[4], GROUPS)).reshape((GROUPS, USERS)).astype(jnp.int32)
    gain = jnp.clip(1.0 + 0.18 * jax.random.normal(streams_of[5], (D,), jnp.float32), 0.1, 1.9)
    grad_out = noise(streams_of[6], (GROUPS, SEQLEN, D), 1.0, 6.0, ((0, 8), (1, 4)))
    return {"queries": queries, "keys": keys, "values": values, "gates": gates, "lengths": lengths, "gain": gain, "grad_out": grad_out}


def positions_info(pos, lens):
    ends = jnp.cumsum(lens)
    seg = lax.optimization_barrier(jnp.sum((pos[:, None] >= ends[None, :]).astype(jnp.int32), axis=1))
    users = jnp.arange(lens.shape[0], dtype=jnp.int32)
    span = lax.optimization_barrier(jnp.sum(jnp.where(seg[:, None] == users[None, :], lens[None, :], 0), axis=1))
    return (seg, 1.0 / span.astype(jnp.float32))

def silu_slope(scores):
    sig = jax.nn.sigmoid(scores)
    return sig * (1.0 + scores * (1.0 - sig))

def reference(queries, keys, values, gates, lengths, gain, grad_out):

    def one_group(item):
        query, key, value, gate, lens, grad = item
        seq_len, width = query.shape
        head_size = width // H
        scale = 1.0 / math.sqrt(head_size)
        pos = jnp.arange(seq_len, dtype=jnp.int32)
        seg, inverse = positions_info(pos, lens)
        allowed = (seg[:, None] == seg[None, :]) & (pos[None, :] <= pos[:, None])
        weight = jnp.where(allowed, inverse[:, None], jnp.float32(0.0))
        q3 = query.astype(jnp.float32).reshape(seq_len, H, head_size)
        k3 = key.astype(jnp.float32).reshape(seq_len, H, head_size)
        v3 = value.astype(jnp.float32).reshape(seq_len, H, head_size)
        scores = jnp.einsum('thd,shd->hts', q3, k3) * scale
        probs = (jax.nn.silu(scores) * weight[None]).astype(jnp.bfloat16)
        attended = jnp.einsum('hts,shd->thd', probs.astype(jnp.float32), v3).reshape(seq_len, width)
        center = attended - lax.optimization_barrier(jnp.mean(attended, axis=1, keepdims=True))
        rstd = lax.rsqrt(lax.optimization_barrier(jnp.mean(center * center, axis=1, keepdims=True)) + 1e-05)
        normed = center * rstd
        gate_f = gate.astype(jnp.float32)
        grad_f = grad.astype(jnp.float32)
        output = (normed * gain[None, :] * gate_f).astype(jnp.bfloat16)
        grad_gate = (grad_f * normed * gain[None, :]).astype(jnp.bfloat16)
        gain_part = lax.optimization_barrier(jnp.sum(grad_f * gate_f * normed, axis=0))
        dnorm = grad_f * gate_f * gain[None, :]
        grad_att = rstd * (dnorm - lax.optimization_barrier(jnp.mean(dnorm, axis=1, keepdims=True)) - normed * lax.optimization_barrier(jnp.mean(dnorm * normed, axis=1, keepdims=True)))
        grad_att = grad_att.astype(jnp.bfloat16)
        ga3 = grad_att.astype(jnp.float32).reshape(seq_len, H, head_size)
        grad_probs = jnp.einsum('thd,shd->hts', ga3, v3)
        grad_scores = (grad_probs * weight[None] * silu_slope(scores)).astype(jnp.bfloat16)
        gs = grad_scores.astype(jnp.float32)
        grad_q = (jnp.einsum('hts,shd->thd', gs, k3) * scale).reshape(seq_len, width).astype(jnp.bfloat16)
        grad_k = (jnp.einsum('hts,thd->shd', gs, q3) * scale).reshape(seq_len, width).astype(jnp.bfloat16)
        grad_v = jnp.einsum('hts,thd->shd', probs.astype(jnp.float32), ga3).reshape(seq_len, width).astype(jnp.bfloat16)
        return (output, grad_q, grad_k, grad_v, grad_gate, gain_part)
    results = lax.map(one_group, (queries, keys, values, gates, lengths, grad_out))
    grad_gain = lax.optimization_barrier(jnp.sum(results[5], axis=0))
    return (results[0], results[1], results[2], results[3], results[4], grad_gain)
```

```python
import functools
import math

import jax
import jax.numpy as jnp
from jax import lax
from jax.experimental import pallas as pl
from jax.experimental.pallas import tpu as pltpu
from jax.sharding import PartitionSpec as P

H = 8
MESH = pl.DeviceIdType.MESH
K, V, Q, G = 0, 1, 2, 3


def dot_nt(a, b):
    return lax.dot_general(a, b, (((1,), (1,)), ((), ())), preferred_element_type=jnp.float32)


def dot_nn(a, b):
    return lax.dot_general(a, b, (((1,), (0,)), ((), ())), preferred_element_type=jnp.float32)


def silu_and_slope(scores):
    sig = 0.5 * jnp.tanh(0.5 * scores) + 0.5
    silu = scores * sig
    return silu, sig + silu * (1.0 - sig)


def kernel(
    n, m, reach, scale,
    lens_ref, gain_ref, q_hbm, k_hbm, v_hbm, gate_hbm, grad_hbm,
    out_hbm, gq_hbm, gk_hbm, gv_hbm, gg_hbm, ggain_ref,
    blocks, gate, grad, row_probs, row_slope, col_probs, col_slope,
    attended, gq_sum, gk_sum, gv_sum, results,
    part, seq_parts, total, own_parts,
    load_sem, store_sem, send_sem, recv_sem, seq_send, seq_recv, own_send, own_recv,
):
    me = lax.axis_index("seq")
    mine = lax.axis_index("own")
    rows, width = gate.shape
    head = width // H
    users = lens_ref.shape[1]
    hbm = {K: k_hbm, V: v_hbm, Q: q_hbm}

    def cols(h):
        return slice(h * head, (h + 1) * head)

    def steps(low, body):
        if reach <= 3:
            for d in range(low, reach + 1):
                body(d)
        else:
            pl.loop(low, reach + 1)(body)

    def load(i, src, dst):
        return pltpu.make_async_copy(src, dst, load_sem.at[i])

    loads = [
        load(0, q_hbm.at[0], blocks.at[Q, 0]),
        load(1, k_hbm.at[0], blocks.at[K, 0]),
        load(2, v_hbm.at[0], blocks.at[V, 0]),
        load(3, gate_hbm.at[0], gate),
        load(4, grad_hbm.at[0], grad),
    ]
    for copy in loads:
        copy.start()

    barrier = pltpu.get_barrier_semaphore()

    @pl.loop(1, n)
    def _(j):
        pl.semaphore_signal(barrier, 1, device_id={"seq": lax.rem(me + j, n)}, device_id_type=MESH)

    @pl.loop(1, m)
    def _(j):
        pl.semaphore_signal(barrier, 1, device_id={"own": lax.rem(mine + j, m)}, device_id_type=MESH)

    pl.semaphore_wait(barrier, n + m - 2)

    def send(what, d):
        peer = me + d if what in (K, V) else me - d
        src = blocks.at[G, 0] if what == G else hbm[what].at[0]
        return pltpu.make_async_remote_copy(
            src_ref=src, dst_ref=blocks.at[what, d],
            send_sem=send_sem.at[what, d], recv_sem=recv_sem.at[what, d],
            device_id={"seq": peer}, device_id_type=MESH,
        )

    def can_send(what, d):
        return me + d < n if what in (K, V) else me >= d

    def start(what):
        def body(d):
            @pl.when(can_send(what, d))
            def _():
                send(what, d).start()
        steps(1, body)

    def wait_sends(what):
        def body(d):
            @pl.when(can_send(what, d))
            def _():
                send(what, d).wait_send()
        steps(1, body)

    start(K)
    start(V)
    start(Q)

    def weight(row_block, col_block, row_dim):
        t = row_block * rows + lax.broadcasted_iota(jnp.int32, (rows, rows), row_dim)
        s = col_block * rows + lax.broadcasted_iota(jnp.int32, (rows, rows), 1 - row_dim)
        first = jnp.zeros_like(t)
        span = jnp.ones_like(t)
        end = jnp.int32(0)
        for u in range(users):
            begin, end = end, end + lens_ref[0, u]
            inside = (t >= begin) & (t < end)
            first = jnp.where(inside, begin, first)
            span = jnp.where(inside, lens_ref[0, u], span)
        inverse = 1.0 / span.astype(jnp.float32)
        return jnp.where((s >= first) & (s <= t), inverse, 0.0)

    for copy in loads[:3]:
        copy.wait()

    def row_scores(d):
        @pl.when(me >= d)
        def _():
            if not isinstance(d, int) or d > 0:
                send(K, d).wait_recv()
            w = weight(me, me - d, 0)
            for h in range(H):
                scores = dot_nt(blocks[Q, 0, :, cols(h)], blocks[K, d, :, cols(h)]) * scale
                silu, slope = silu_and_slope(scores)
                row_probs[d, h] = (silu * w).astype(jnp.bfloat16)
                row_slope[d, h] = slope * w

    def row_attend(d):
        @pl.when(me >= d)
        def _():
            send(V, d).wait_recv()
            for h in range(H):
                attended[:, cols(h)] += dot_nn(row_probs[d, h], blocks[V, d, :, cols(h)])

    row_scores(0)
    for h in range(H):
        attended[:, cols(h)] = dot_nn(row_probs[0, h], blocks[V, 0, :, cols(h)])
    steps(1, row_scores)
    steps(1, row_attend)

    for copy in loads[3:]:
        copy.wait()
    gain = gain_ref[...]
    step = 32 if rows % 32 == 0 else rows
    share = jnp.zeros((1, width), jnp.float32)
    for r in range(0, rows, step):
        at = slice(r, r + step)
        att = attended[at, :]
        center = att - jnp.mean(att, axis=1, keepdims=True)
        rstd = lax.rsqrt(jnp.mean(center * center, axis=1, keepdims=True) + 1e-05)
        normed = center * rstd
        gate_f = gate[at, :].astype(jnp.float32)
        grad_f = grad[at, :].astype(jnp.float32)
        scaled = normed * gain
        results[0, at, :] = (scaled * gate_f).astype(jnp.bfloat16)
        results[1, at, :] = (grad_f * scaled).astype(jnp.bfloat16)
        both = grad_f * gate_f
        share = share + jnp.sum(both * normed, axis=0, keepdims=True)
        dnorm = both * gain
        back = rstd * (
            dnorm
            - jnp.mean(dnorm, axis=1, keepdims=True)
            - normed * jnp.mean(dnorm * normed, axis=1, keepdims=True)
        )
        blocks[G, 0, at, :] = back.astype(jnp.bfloat16)
    start(G)
    part[...] = share

    def seq_share(j):
        return pltpu.make_async_remote_copy(
            src_ref=part, dst_ref=seq_parts.at[me],
            send_sem=seq_send.at[j], recv_sem=seq_recv.at[me],
            device_id={"seq": lax.rem(me + j, n)}, device_id_type=MESH,
        )

    def own_share(j):
        return pltpu.make_async_remote_copy(
            src_ref=total, dst_ref=own_parts.at[mine],
            send_sem=own_send.at[j], recv_sem=own_recv.at[mine],
            device_id={"own": lax.rem(mine + j, m)}, device_id_type=MESH,
        )

    pl.loop(1, n)(lambda j: seq_share(j).start())
    seq_parts[me] = share

    def store(i, dst):
        return pltpu.make_async_copy(results.at[i], dst.at[0], store_sem.at[i])

    stores = [store(i, dst) for i, dst in enumerate((out_hbm, gg_hbm, gq_hbm, gk_hbm, gv_hbm))]
    stores[0].start()
    stores[1].start()

    def row_back(d):
        @pl.when(me >= d)
        def _():
            for h in range(H):
                grad_probs = dot_nt(blocks[G, 0, :, cols(h)], blocks[V, d, :, cols(h)])
                grad_scores = (grad_probs * row_slope[d, h]).astype(jnp.bfloat16)
                term = dot_nn(grad_scores, blocks[K, d, :, cols(h)])
                if isinstance(d, int) and d == 0:
                    gq_sum[:, cols(h)] = term
                else:
                    gq_sum[:, cols(h)] += term

    row_back(0)
    steps(1, row_back)
    results[2] = (gq_sum[...] * scale).astype(jnp.bfloat16)
    stores[2].start()

    @pl.loop(1, n)
    def _(j):
        src = lax.rem(me + j, n)
        pltpu.make_async_remote_copy(
            src_ref=part, dst_ref=seq_parts.at[src],
            send_sem=seq_send.at[j], recv_sem=seq_recv.at[src],
            device_id={"seq": src}, device_id_type=MESH,
        ).wait_recv()

    group = seq_parts[0]
    for j in range(1, n):
        group = group + seq_parts[j]
    total[...] = group
    pl.loop(1, m)(lambda j: own_share(j).start())
    own_parts[mine] = group

    def col_scores(d):
        @pl.when(me + d < n)
        def _():
            if not isinstance(d, int) or d > 0:
                send(Q, d).wait_recv()
            w = weight(me + d, me, 1)
            for h in range(H):
                scores = dot_nt(blocks[K, 0, :, cols(h)], blocks[Q, d, :, cols(h)]) * scale
                silu, slope = silu_and_slope(scores)
                col_probs[d, h] = (silu * w).astype(jnp.bfloat16)
                col_slope[d, h] = slope * w

    def col_back(d):
        @pl.when(me + d < n)
        def _():
            own = isinstance(d, int) and d == 0
            if not own:
                send(G, d).wait_recv()
            for h in range(H):
                back = blocks[G, d, :, cols(h)]
                grad_probs = dot_nt(blocks[V, 0, :, cols(h)], back)
                grad_scores = (grad_probs * col_slope[d, h]).astype(jnp.bfloat16)
                key_term = dot_nn(grad_scores, blocks[Q, d, :, cols(h)])
                value_term = dot_nn(col_probs[d, h], back)
                if own:
                    gk_sum[:, cols(h)] = key_term
                    gv_sum[:, cols(h)] = value_term
                else:
                    gk_sum[:, cols(h)] += key_term
                    gv_sum[:, cols(h)] += value_term

    col_scores(0)
    steps(1, col_scores)
    col_back(0)
    steps(1, col_back)
    results[3] = (gk_sum[...] * scale).astype(jnp.bfloat16)
    results[4] = gv_sum[...].astype(jnp.bfloat16)
    stores[3].start()
    stores[4].start()

    @pl.loop(1, m)
    def _(j):
        src = lax.rem(mine + j, m)
        pltpu.make_async_remote_copy(
            src_ref=total, dst_ref=own_parts.at[src],
            send_sem=own_send.at[j], recv_sem=own_recv.at[src],
            device_id={"own": src}, device_id_type=MESH,
        ).wait_recv()

    whole = own_parts[0]
    for j in range(1, m):
        whole = whole + own_parts[j]
    ggain_ref[...] = whole

    for what in (K, V, Q, G):
        wait_sends(what)
    pl.loop(1, n)(lambda j: seq_share(j).wait_send())
    pl.loop(1, m)(lambda j: own_share(j).wait_send())
    for copy in stores:
        copy.wait()


def per_device(n, m, queries, keys, values, gates, lengths, gain, grad_out):
    rows, width = queries.shape[1], queries.shape[2]
    head = width // H
    reach = min(n - 1, (rows * n // 2 - 1) // rows + 1)
    slots = reach + 1
    any_spec = pl.BlockSpec(memory_space=pl.ANY)
    vmem = pl.BlockSpec(memory_space=pltpu.VMEM)
    block = jax.ShapeDtypeStruct(queries.shape, jnp.bfloat16)
    dma = pltpu.SemaphoreType.DMA
    outs = pl.pallas_call(
        functools.partial(kernel, n, m, reach, 1.0 / math.sqrt(head)),
        out_shape=[block] * 5 + [jax.ShapeDtypeStruct((1, width), jnp.float32)],
        in_specs=[pl.BlockSpec(memory_space=pltpu.SMEM), vmem] + [any_spec] * 5,
        out_specs=[any_spec] * 5 + [vmem],
        scratch_shapes=[
            pltpu.VMEM((4, slots, rows, width), jnp.bfloat16),
            pltpu.VMEM((rows, width), jnp.bfloat16),
            pltpu.VMEM((rows, width), jnp.bfloat16),
            pltpu.VMEM((slots, H, rows, rows), jnp.bfloat16),
            pltpu.VMEM((slots, H, rows, rows), jnp.float32),
            pltpu.VMEM((slots, H, rows, rows), jnp.bfloat16),
            pltpu.VMEM((slots, H, rows, rows), jnp.float32),
            pltpu.VMEM((rows, width), jnp.float32),
            pltpu.VMEM((rows, width), jnp.float32),
            pltpu.VMEM((rows, width), jnp.float32),
            pltpu.VMEM((rows, width), jnp.float32),
            pltpu.VMEM((5, rows, width), jnp.bfloat16),
            pltpu.VMEM((1, width), jnp.float32),
            pltpu.VMEM((n, 1, width), jnp.float32),
            pltpu.VMEM((1, width), jnp.float32),
            pltpu.VMEM((m, 1, width), jnp.float32),
            dma((5,)), dma((5,)), dma((4, slots)), dma((4, slots)),
            dma((n,)), dma((n,)), dma((m,)), dma((m,)),
        ],
        compiler_params=pltpu.CompilerParams(
            collective_id=0, has_side_effects=True, vmem_limit_bytes=44 * 1024 * 1024
        ),
        cost_estimate=pl.CostEstimate(
            flops=16 * slots * rows * rows * width, bytes_accessed=20 * rows * width, transcendentals=0
        ),
    )(lengths, gain.reshape(1, width), queries, keys, values, gates, grad_out)
    output, grad_q, grad_k, grad_v, grad_gate, grad_gain = outs
    return output, grad_q, grad_k, grad_v, grad_gate, grad_gain.reshape(width)


def solution(mesh):
    blocked = P("own", "seq", None)
    sizes = (mesh.shape["seq"], mesh.shape["own"])
    return jax.shard_map(
        functools.partial(per_device, *sizes),
        mesh=mesh,
        in_specs=(blocked, blocked, blocked, blocked, P("own", None), P(), blocked),
        out_specs=(blocked, blocked, blocked, blocked, blocked, P()),
        check_vma=False,
    )
```

```python
import functools
import math

import jax
import jax.numpy as jnp
from jax import lax
from jax.experimental import pallas as pl
from jax.experimental.pallas import tpu as pltpu
from jax.sharding import PartitionSpec as P

H = 8
MESH = pl.DeviceIdType.MESH
K, V, Q, G = 0, 1, 2, 3
PIECES = 2
ROOM = 60 * 1024 * 1024


def dot_nt(a, b):
    return lax.dot_general(a, b, (((1,), (1,)), ((), ())), preferred_element_type=jnp.float32)


def dot_nn(a, b):
    return lax.dot_general(a, b, (((1,), (0,)), ((), ())), preferred_element_type=jnp.float32)


def silu_and_slope(scores):
    sig = 0.5 * jnp.tanh(0.5 * scores) + 0.5
    silu = scores * sig
    return silu, sig + silu * (1.0 - sig)


def kernel(
    n, m, reach, scale,
    lens_hbm, gain_hbm, q_hbm, k_hbm, v_hbm, gate_hbm, grad_hbm,
    out_hbm, gq_hbm, gk_hbm, gv_hbm, gg_hbm, ggain_hbm,
    lens_ref, gain_ref, blocks, gate, grad, row_probs, row_slope, col_probs, col_slope,
    attended, gq_sum, gk_sum, gv_sum, results,
    part, seq_parts, total, own_parts, part_sum,
    load_sem, store_sem, send_sem, recv_sem, relay_sem, seq_send, seq_recv, own_send, own_recv,
):
    me = lax.axis_index("seq")
    mine = lax.axis_index("own")
    rows, width = gate.shape
    head = width // H
    users = lens_ref.shape[1]
    hbm = {K: k_hbm, V: v_hbm, Q: q_hbm}
    relayed = n == 4 and reach == 2
    piece = rows // PIECES

    def cols(h):
        return slice(h * head, (h + 1) * head)

    def steps(low, body):
        if reach <= 3:
            for d in range(low, reach + 1):
                body(d)
        else:
            pl.loop(low, reach + 1)(body)

    def load(i, src, dst):
        return pltpu.make_async_copy(src, dst, load_sem.at[i])

    loads = [
        load(0, q_hbm.at[0], blocks.at[Q, 0]),
        load(1, k_hbm.at[0], blocks.at[K, 0]),
        load(2, v_hbm.at[0], blocks.at[V, 0]),
        load(3, gate_hbm.at[0], gate),
        load(4, grad_hbm.at[0], grad),
        load(5, gain_hbm, gain_ref),
        load(6, lens_hbm, lens_ref),
    ]
    for copy in loads:
        copy.start()

    barrier = pltpu.get_barrier_semaphore()

    @pl.loop(1, n)
    def _(j):
        pl.semaphore_signal(barrier, 1, device_id={"seq": lax.rem(me + j, n)}, device_id_type=MESH)

    @pl.loop(1, m)
    def _(j):
        pl.semaphore_signal(barrier, 1, device_id={"own": lax.rem(mine + j, m)}, device_id_type=MESH)

    pl.semaphore_wait(barrier, n + m - 2)

    def later(what):
        return what in (K, V)

    def span(c):
        return pl.ds(c * piece, piece)

    def send(what, d, c):
        src = blocks.at[G, 0, span(c)] if what == G else hbm[what].at[0, span(c)]
        return pltpu.make_async_remote_copy(
            src_ref=src, dst_ref=blocks.at[what, d, span(c)],
            send_sem=send_sem.at[what, d, c], recv_sem=recv_sem.at[what, d, c],
            device_id={"seq": me + d if later(what) else me - d}, device_id_type=MESH,
        )

    def relay(what, c):
        return pltpu.make_async_remote_copy(
            src_ref=blocks.at[what, 2, span(c)], dst_ref=blocks.at[what, 1, span(c)],
            send_sem=relay_sem.at[what, c], recv_sem=recv_sem.at[what, 1, c],
            device_id={"seq": 2 if later(what) else 1}, device_id_type=MESH,
        )

    def can_send(what, d):
        ok = me + d < n if later(what) else me >= d
        if relayed and d == 1:
            ok = ok & (me != (1 if later(what) else 2))
        return ok

    def start(what, pieces):
        def body(d):
            @pl.when(can_send(what, d))
            def _():
                for c in pieces:
                    send(what, d, c).start()
        steps(1, body)

    def wait_sends(what):
        def body(d):
            @pl.when(can_send(what, d))
            def _():
                for c in range(PIECES):
                    send(what, d, c).wait_send()
        steps(1, body)

    def arrive(what, d):
        for c in range(PIECES):
            send(what, d, c).wait_recv()

    def arrive_and_relay(what):
        for c in range(PIECES):
            send(what, 2, c).wait_recv()
            relay(what, c).start()

    everything = range(PIECES)
    start(K, everything)
    start(V, everything)
    if relayed:
        @pl.when(me != 3)
        def _():
            start(Q, everything)

        @pl.when(me == 3)
        def _():
            for c in everything:
                send(Q, 2, c).start()
    else:
        start(Q, everything)

    def weight(row_block, col_block, row_dim):
        t = row_block * rows + lax.broadcasted_iota(jnp.int32, (rows, rows), row_dim)
        s = col_block * rows + lax.broadcasted_iota(jnp.int32, (rows, rows), 1 - row_dim)
        first = jnp.zeros_like(t)
        span = jnp.ones_like(t)
        end = jnp.int32(0)
        for u in range(users):
            begin, end = end, end + lens_ref[0, u]
            inside = (t >= begin) & (t < end)
            first = jnp.where(inside, begin, first)
            span = jnp.where(inside, lens_ref[0, u], span)
        inverse = 1.0 / span.astype(jnp.float32)
        return jnp.where((s >= first) & (s <= t), inverse, 0.0)

    for copy in loads[:3] + loads[5:]:
        copy.wait()

    def row_scores(d):
        @pl.when(me >= d)
        def _():
            w = weight(me, me - d, 0)
            for h in range(H):
                scores = dot_nt(blocks[Q, 0, :, cols(h)], blocks[K, d, :, cols(h)]) * scale
                silu, slope = silu_and_slope(scores)
                row_probs[d, h] = (silu * w).astype(jnp.bfloat16)
                row_slope[d, h] = slope * w

    def row_attend(d):
        @pl.when(me >= d)
        def _():
            for h in range(H):
                attended[:, cols(h)] += dot_nn(row_probs[d, h], blocks[V, d, :, cols(h)])

    def row_arrive(what):
        if relayed:
            @pl.when(me == 3)
            def _():
                arrive_and_relay(what)
                arrive(what, 1)

            @pl.when((me > 0) & (me < 3))
            def _():
                arrive(what, 1)

            @pl.when(me == 2)
            def _():
                arrive(what, 2)
        else:
            def body(d):
                @pl.when(me >= d)
                def _():
                    arrive(what, d)
            steps(1, body)

    row_scores(0)
    for h in range(H):
        attended[:, cols(h)] = dot_nn(row_probs[0, h], blocks[V, 0, :, cols(h)])
    row_arrive(K)
    steps(1, row_scores)
    row_arrive(V)
    if relayed:
        @pl.when(me == 3)
        def _():
            for c in everything:
                send(Q, 1, c).start()
    steps(1, row_attend)

    for copy in loads[3:5]:
        copy.wait()
    gain = gain_ref[...]
    step = 32 if piece % 32 == 0 else piece
    for c in everything:
        for r in range(c * piece, (c + 1) * piece, step):
            at = slice(r, r + step)
            att = attended[at, :]
            center = att - jnp.mean(att, axis=1, keepdims=True)
            rstd = lax.rsqrt(jnp.mean(center * center, axis=1, keepdims=True) + 1e-05)
            normed = center * rstd
            dnorm = grad[at, :].astype(jnp.float32) * gate[at, :].astype(jnp.float32) * gain
            back = rstd * (
                dnorm
                - jnp.mean(dnorm, axis=1, keepdims=True)
                - normed * jnp.mean(dnorm * normed, axis=1, keepdims=True)
            )
            attended[at, :] = normed
            blocks[G, 0, at, :] = back.astype(jnp.bfloat16)
        start(G, [c])

    share = jnp.zeros((1, width), jnp.float32)
    for r in range(0, rows, step):
        at = slice(r, r + step)
        normed = attended[at, :]
        gate_f = gate[at, :].astype(jnp.float32)
        grad_f = grad[at, :].astype(jnp.float32)
        results[0, at, :] = (normed * gain * gate_f).astype(jnp.bfloat16)
        results[1, at, :] = (grad_f * normed * gain).astype(jnp.bfloat16)
        share = share + jnp.sum(grad_f * gate_f * normed, axis=0, keepdims=True)
    part[...] = share

    def seq_share(j):
        return pltpu.make_async_remote_copy(
            src_ref=part, dst_ref=seq_parts.at[me],
            send_sem=seq_send.at[j], recv_sem=seq_recv.at[me],
            device_id={"seq": lax.rem(me + j, n)}, device_id_type=MESH,
        )

    def own_share(j):
        return pltpu.make_async_remote_copy(
            src_ref=total, dst_ref=own_parts.at[mine],
            send_sem=own_send.at[j], recv_sem=own_recv.at[mine],
            device_id={"own": lax.rem(mine + j, m)}, device_id_type=MESH,
        )

    pl.loop(1, n)(lambda j: seq_share(j).start())
    seq_parts[me] = share

    def store(i, dst):
        return pltpu.make_async_copy(results.at[i], dst.at[0], store_sem.at[i])

    if relayed:
        @pl.when(me == 0)
        def _():
            arrive_and_relay(Q)

    stores = [store(i, dst) for i, dst in enumerate((out_hbm, gg_hbm, gq_hbm, gk_hbm, gv_hbm))]
    stores[0].start()
    stores[1].start()

    def row_back(d):
        @pl.when(me >= d)
        def _():
            for h in range(H):
                grad_probs = dot_nt(blocks[G, 0, :, cols(h)], blocks[V, d, :, cols(h)])
                grad_scores = (grad_probs * row_slope[d, h]).astype(jnp.bfloat16)
                term = dot_nn(grad_scores, blocks[K, d, :, cols(h)])
                if isinstance(d, int) and d == 0:
                    gq_sum[:, cols(h)] = term
                else:
                    gq_sum[:, cols(h)] += term

    row_back(0)
    steps(1, row_back)
    results[2] = (gq_sum[...] * scale).astype(jnp.bfloat16)
    stores[2].start()

    @pl.loop(1, n)
    def _(j):
        src = lax.rem(me + j, n)
        pltpu.make_async_remote_copy(
            src_ref=part, dst_ref=seq_parts.at[src],
            send_sem=seq_send.at[j], recv_sem=seq_recv.at[src],
            device_id={"seq": src}, device_id_type=MESH,
        ).wait_recv()

    group = seq_parts[0]
    for j in range(1, n):
        group = group + seq_parts[j]
    total[...] = group
    pl.loop(1, m)(lambda j: own_share(j).start())
    own_parts[mine] = group

    def col_scores(d):
        @pl.when(me + d < n)
        def _():
            if not isinstance(d, int):
                arrive(Q, d)
            elif d == 2 and relayed:
                pl.when(me != 0)(lambda: arrive(Q, d))
            elif d > 0:
                arrive(Q, d)
            w = weight(me + d, me, 1)
            for h in range(H):
                scores = dot_nt(blocks[K, 0, :, cols(h)], blocks[Q, d, :, cols(h)]) * scale
                silu, slope = silu_and_slope(scores)
                col_probs[d, h] = (silu * w).astype(jnp.bfloat16)
                col_slope[d, h] = slope * w

    def col_back(d):
        @pl.when(me + d < n)
        def _():
            own = isinstance(d, int) and d == 0
            if not own and not (relayed and d == 2):
                arrive(G, d)
            for h in range(H):
                back = blocks[G, d, :, cols(h)]
                grad_probs = dot_nt(blocks[V, 0, :, cols(h)], back)
                grad_scores = (grad_probs * col_slope[d, h]).astype(jnp.bfloat16)
                key_term = dot_nn(grad_scores, blocks[Q, d, :, cols(h)])
                value_term = dot_nn(col_probs[d, h], back)
                if own:
                    gk_sum[:, cols(h)] = key_term
                    gv_sum[:, cols(h)] = value_term
                else:
                    gk_sum[:, cols(h)] += key_term
                    gv_sum[:, cols(h)] += value_term

    col_scores(0)
    steps(1, col_scores)
    col_back(0)
    if relayed:
        @pl.when(me == 0)
        def _():
            arrive_and_relay(G)

        @pl.when(me == 1)
        def _():
            arrive(G, 2)

        col_back(2)
        col_back(1)
    else:
        steps(1, col_back)
    results[3] = (gk_sum[...] * scale).astype(jnp.bfloat16)
    results[4] = gv_sum[...].astype(jnp.bfloat16)
    stores[3].start()
    stores[4].start()

    @pl.loop(1, m)
    def _(j):
        src = lax.rem(mine + j, m)
        pltpu.make_async_remote_copy(
            src_ref=total, dst_ref=own_parts.at[src],
            send_sem=own_send.at[j], recv_sem=own_recv.at[src],
            device_id={"own": src}, device_id_type=MESH,
        ).wait_recv()

    whole = own_parts[0]
    for j in range(1, m):
        whole = whole + own_parts[j]
    part_sum[...] = whole
    last = pltpu.make_async_copy(part_sum, ggain_hbm, store_sem.at[5])
    last.start()

    for what in (K, V, Q, G):
        wait_sends(what)
    if relayed:
        for what in (K, V, Q, G):
            @pl.when(me == (3 if later(what) else 0))
            def _():
                for c in everything:
                    relay(what, c).wait_send()
    pl.loop(1, n)(lambda j: seq_share(j).wait_send())
    pl.loop(1, m)(lambda j: own_share(j).wait_send())
    for copy in stores + [last]:
        copy.wait()


def finish(*refs):
    sources, results, sem = refs[:6], refs[6:12], refs[12]
    copies = [pltpu.make_async_copy(a, b, sem.at[i]) for i, (a, b) in enumerate(zip(sources, results))]
    for copy in copies:
        copy.start()
    for copy in copies:
        copy.wait()


def per_device(n, m, queries, keys, values, gates, lengths, gain, grad_out):
    rows, width = queries.shape[1], queries.shape[2]
    head = width // H
    reach = min(n - 1, (rows * n // 2 - 1) // rows + 1)
    slots = reach + 1
    hbm = pl.BlockSpec(memory_space=pltpu.HBM)
    any_spec = pl.BlockSpec(memory_space=pl.ANY)
    block = jax.ShapeDtypeStruct(queries.shape, jnp.bfloat16)
    shapes = [block] * 5 + [jax.ShapeDtypeStruct((1, width), jnp.float32)]
    dma = pltpu.SemaphoreType.DMA
    outs = pl.pallas_call(
        functools.partial(kernel, n, m, reach, 1.0 / math.sqrt(head)),
        out_shape=shapes,
        in_specs=[hbm] * 7,
        out_specs=[any_spec] * 6,
        scratch_shapes=[
            pltpu.SMEM(lengths.shape, jnp.int32),
            pltpu.VMEM((1, width), jnp.float32),
            pltpu.VMEM((4, slots, rows, width), jnp.bfloat16),
            pltpu.VMEM((rows, width), jnp.bfloat16),
            pltpu.VMEM((rows, width), jnp.bfloat16),
            pltpu.VMEM((slots, H, rows, rows), jnp.bfloat16),
            pltpu.VMEM((slots, H, rows, rows), jnp.float32),
            pltpu.VMEM((slots, H, rows, rows), jnp.bfloat16),
            pltpu.VMEM((slots, H, rows, rows), jnp.float32),
            pltpu.VMEM((rows, width), jnp.float32),
            pltpu.VMEM((rows, width), jnp.float32),
            pltpu.VMEM((rows, width), jnp.float32),
            pltpu.VMEM((rows, width), jnp.float32),
            pltpu.VMEM((5, rows, width), jnp.bfloat16),
            pltpu.VMEM((1, width), jnp.float32),
            pltpu.VMEM((n, 1, width), jnp.float32),
            pltpu.VMEM((1, width), jnp.float32),
            pltpu.VMEM((m, 1, width), jnp.float32),
            pltpu.VMEM((1, width), jnp.float32),
            dma((7,)), dma((6,)), dma((4, slots, PIECES)), dma((4, slots, PIECES)), dma((4, PIECES)),
            dma((n,)), dma((n,)), dma((m,)), dma((m,)),
        ],
        compiler_params=pltpu.CompilerParams(
            collective_id=0, has_side_effects=True, vmem_limit_bytes=ROOM
        ),
        cost_estimate=pl.CostEstimate(
            flops=16 * slots * rows * rows * width, bytes_accessed=20 * rows * width, transcendentals=0
        ),
    )(lengths, gain.reshape(1, width), queries, keys, values, gates, grad_out)
    output, grad_q, grad_k, grad_v, grad_gate, grad_gain = pl.pallas_call(
        finish,
        out_shape=shapes,
        in_specs=[any_spec] * 6,
        out_specs=[any_spec] * 6,
        scratch_shapes=[dma((6,))],
        compiler_params=pltpu.CompilerParams(has_side_effects=True, vmem_limit_bytes=ROOM),
    )(*outs)
    return output, grad_q, grad_k, grad_v, grad_gate, grad_gain.reshape(width)


def solution(mesh):
    blocked = P("own", "seq", None)
    sizes = (mesh.shape["seq"], mesh.shape["own"])
    return jax.shard_map(
        functools.partial(per_device, *sizes),
        mesh=mesh,
        in_specs=(blocked, blocked, blocked, blocked, P("own", None), P(), blocked),
        out_specs=(blocked, blocked, blocked, blocked, blocked, P()),
        check_vma=False,
    )
```

```python
import functools
import math

import jax
import jax.numpy as jnp
from jax import lax
from jax.experimental import pallas as pl
from jax.experimental.pallas import tpu as pltpu
from jax.sharding import PartitionSpec as P

H = 8
MESH = pl.DeviceIdType.MESH
K, V, Q, G = 0, 1, 2, 3
PIECES = 2
ROOM = 60 * 1024 * 1024


def dot_nt(a, b):
    return lax.dot_general(a, b, (((1,), (1,)), ((), ())), preferred_element_type=jnp.float32)


def dot_nn(a, b):
    return lax.dot_general(a, b, (((1,), (0,)), ((), ())), preferred_element_type=jnp.float32)


def silu_and_slope(scores):
    sig = 0.5 * jnp.tanh(0.5 * scores) + 0.5
    silu = scores * sig
    return silu, sig + silu * (1.0 - sig)


def kernel(
    n, m, reach, wide, scale,
    lens_hbm, gain_hbm, q_hbm, k_hbm, v_hbm, gate_hbm, grad_hbm,
    out_hbm, gq_hbm, gk_hbm, gv_hbm, gg_hbm, ggain_hbm,
    lens_ref, gain_ref, blocks, gate, grad,
    row_probs, row_slope, col_probs, col_slope,
    far_row_probs, far_row_slope, far_col_probs, far_col_slope,
    attended, gq_sum, gk_sum, gv_sum, results,
    part, seq_parts, total, own_parts, part_sum,
    load_sem, store_sem, send_sem, recv_sem, relay_sem, seq_send, seq_recv, own_send, own_recv,
):
    me = lax.axis_index("seq")
    mine = lax.axis_index("own")
    rows, width = gate.shape
    head = width // H
    users = lens_ref.shape[1]
    groups = reach // wide
    relayed = n == 4 and reach == 2
    piece = rows // PIECES
    everything = range(PIECES)

    def near(what, h):
        return blocks[what, 0, :, h]

    def far(what, first, h):
        return blocks[what, pl.ds(first, wide), :, h].reshape(wide * rows, head)

    def each_head(count, body):
        @pl.loop(0, H // count)
        def _(i):
            for j in range(count):
                h = i * count + j
                body(h, pl.ds(pl.multiple_of(h * head, head), head))

    def load(i, src, dst):
        return pltpu.make_async_copy(src, dst, load_sem.at[i])

    loads = [
        load(0, k_hbm.at[0], blocks.at[K, 0]),
        load(1, v_hbm.at[0], blocks.at[V, 0]),
        load(2, q_hbm.at[0], blocks.at[Q, 0]),
        load(3, gate_hbm.at[0], gate),
        load(4, grad_hbm.at[0], grad),
        load(5, gain_hbm, gain_ref),
        load(6, lens_hbm, lens_ref),
    ]
    for copy in loads:
        copy.start()

    barrier = pltpu.get_barrier_semaphore()

    @pl.loop(1, n)
    def _(j):
        pl.semaphore_signal(barrier, 1, device_id={"seq": lax.rem(me + j, n)}, device_id_type=MESH)

    @pl.loop(1, m)
    def _(j):
        pl.semaphore_signal(barrier, 1, device_id={"own": lax.rem(mine + j, m)}, device_id_type=MESH)

    for copy in loads[:3]:
        copy.wait()
    pl.semaphore_wait(barrier, n + m - 2)

    def later(what):
        return what in (K, V)

    def span(c):
        return pl.ds(c * piece, piece)

    def send(what, d, c):
        return pltpu.make_async_remote_copy(
            src_ref=blocks.at[what, 0, span(c)], dst_ref=blocks.at[what, d, span(c)],
            send_sem=send_sem.at[what, d, c], recv_sem=recv_sem.at[what, d, c],
            device_id={"seq": me + d if later(what) else me - d}, device_id_type=MESH,
        )

    def relay(what, c):
        return pltpu.make_async_remote_copy(
            src_ref=blocks.at[what, 2, span(c)], dst_ref=blocks.at[what, 1, span(c)],
            send_sem=relay_sem.at[what, c], recv_sem=recv_sem.at[what, 1, c],
            device_id={"seq": 2 if later(what) else 1}, device_id_type=MESH,
        )

    def can_send(what, d):
        ok = me + d < n if later(what) else me >= d
        if relayed and d == 1:
            ok = ok & (me != (1 if later(what) else 2))
        return ok

    def start(what, pieces):
        for d in range(1, reach + 1):
            @pl.when(can_send(what, d))
            def _():
                for c in pieces:
                    send(what, d, c).start()

    def wait_sends(what):
        for d in range(1, reach + 1):
            @pl.when(can_send(what, d))
            def _():
                for c in everything:
                    send(what, d, c).wait_send()

    def arrive(what, d):
        for c in everything:
            send(what, d, c).wait_recv()

    def arrive_and_relay(what):
        for c in everything:
            send(what, 2, c).wait_recv()
            relay(what, c).start()

    def arrive_group(what, first):
        for d in range(first, first + wide):
            pl.when(me >= d if later(what) else me + d < n)(functools.partial(arrive, what, d))

    def arrive_all(what):
        if relayed:
            relayer = 3 if later(what) else 0

            @pl.when(me == relayer)
            def _():
                arrive_and_relay(what)
                arrive(what, 1)

            pl.when(me != relayer)(functools.partial(arrive_group, what, 1))

    start(K, everything)
    start(V, everything)
    if relayed:
        pl.when(me != 3)(functools.partial(start, Q, everything))

        @pl.when(me == 3)
        def _():
            for c in everything:
                send(Q, 2, c).start()
    else:
        start(Q, everything)

    if wide == 2:
        for d in range(2, reach + 1, 2):
            @pl.when(me == d - 1)
            def _():
                blocks[K, d] = jnp.zeros((rows, width), jnp.bfloat16)
                blocks[V, d] = jnp.zeros((rows, width), jnp.bfloat16)

            @pl.when(me + d == n)
            def _():
                blocks[Q, d] = jnp.zeros((rows, width), jnp.bfloat16)
                blocks[G, d] = jnp.zeros((rows, width), jnp.bfloat16)

    def weight(t, s):
        first = jnp.zeros_like(t)
        length = jnp.ones_like(t)
        end = jnp.int32(0)
        for u in range(users):
            begin, end = end, end + lens_ref[0, u]
            inside = (t >= begin) & (t < end)
            first = jnp.where(inside, begin, first)
            length = jnp.where(inside, lens_ref[0, u], length)
        return jnp.where((s >= first) & (s <= t), 1.0 / length.astype(jnp.float32), 0.0)

    def iotas(columns):
        return [lax.broadcasted_iota(jnp.int32, (rows, columns), i) for i in (0, 1)]

    for copy in loads[5:]:
        copy.wait()

    def pointwise(scores, w, probs_ref, slope_ref):
        scores = scores * scale
        silu, slope = silu_and_slope(scores)
        probs = (silu * w).astype(jnp.bfloat16)
        probs_ref[...] = probs
        slope_ref[...] = slope * w
        return probs

    down, across = iotas(rows)
    w = weight(me * rows + down, me * rows + across)

    def near_forward(h, at):
        probs = pointwise(dot_nt(near(Q, at), near(K, at)), w, row_probs.at[h], row_slope.at[h])
        attended[:, at] = dot_nn(probs, near(V, at))

    each_head(2, near_forward)

    arrive_all(K)
    for g in range(groups):
        first = 1 + g * wide

        @pl.when(me >= first)
        def _():
            if not relayed:
                arrive_group(K, first)
            down, across = iotas(wide * rows)
            s = (me - first) * rows + across - jnp.where(across >= rows, 2 * rows, 0)
            w = weight(me * rows + down, s)

            def body(h, at):
                scores = dot_nt(near(Q, at), far(K, first, at))
                pointwise(scores, w, far_row_probs.at[g, h], far_row_slope.at[g, h])

            each_head(1, body)

    arrive_all(V)
    if relayed:
        @pl.when(me == 3)
        def _():
            for c in everything:
                send(Q, 1, c).start()
    for g in range(groups):
        first = 1 + g * wide

        @pl.when(me >= first)
        def _():
            if not relayed:
                arrive_group(V, first)

            def body(h, at):
                attended[:, at] += dot_nn(far_row_probs[g, h], far(V, first, at))

            each_head(2, body)

    for copy in loads[3:5]:
        copy.wait()
    gain = gain_ref[...]
    step = 32 if piece % 32 == 0 else piece

    @pl.loop(0, PIECES)
    def _(c):
        for r in range(0, piece, step):
            at = pl.ds(pl.multiple_of(c * piece + r, step), step)
            att = attended[at, :]
            center = att - jnp.mean(att, axis=1, keepdims=True)
            rstd = lax.rsqrt(jnp.mean(center * center, axis=1, keepdims=True) + 1e-05)
            normed = center * rstd
            dnorm = grad[at, :].astype(jnp.float32) * gate[at, :].astype(jnp.float32) * gain
            back = rstd * (
                dnorm
                - jnp.mean(dnorm, axis=1, keepdims=True)
                - normed * jnp.mean(dnorm * normed, axis=1, keepdims=True)
            )
            attended[at, :] = normed
            blocks[G, 0, at, :] = back.astype(jnp.bfloat16)
        start(G, [c])

    part[...] = jnp.zeros((1, width), jnp.float32)

    @pl.loop(0, rows // step)
    def _(i):
        at = pl.ds(pl.multiple_of(i * step, step), step)
        normed = attended[at, :]
        gate_f = gate[at, :].astype(jnp.float32)
        grad_f = grad[at, :].astype(jnp.float32)
        results[0, at, :] = (normed * gain * gate_f).astype(jnp.bfloat16)
        results[1, at, :] = (grad_f * normed * gain).astype(jnp.bfloat16)
        part[...] += jnp.sum(grad_f * gate_f * normed, axis=0, keepdims=True)

    def seq_share(j):
        return pltpu.make_async_remote_copy(
            src_ref=part, dst_ref=seq_parts.at[me],
            send_sem=seq_send.at[j], recv_sem=seq_recv.at[me],
            device_id={"seq": lax.rem(me + j, n)}, device_id_type=MESH,
        )

    def own_share(j):
        return pltpu.make_async_remote_copy(
            src_ref=total, dst_ref=own_parts.at[mine],
            send_sem=own_send.at[j], recv_sem=own_recv.at[mine],
            device_id={"own": lax.rem(mine + j, m)}, device_id_type=MESH,
        )

    pl.loop(1, n)(lambda j: seq_share(j).start())
    seq_parts[me] = part[...]

    def store(i, dst):
        return pltpu.make_async_copy(results.at[i], dst.at[0], store_sem.at[i])

    stores = [store(i, dst) for i, dst in enumerate((out_hbm, gg_hbm, gq_hbm, gk_hbm, gv_hbm))]
    stores[0].start()
    stores[1].start()

    arrive_all(Q)

    down, across = iotas(rows)
    near_w = weight(me * rows + across, me * rows + down)

    def near_column(h, at):
        pointwise(dot_nt(near(K, at), near(Q, at)), near_w, col_probs.at[h], col_slope.at[h])

    each_head(2, near_column)
    for g in range(groups):
        first = 1 + g * wide

        @pl.when(me + first < n)
        def _():
            if not relayed:
                arrive_group(Q, first)
            down, across = iotas(wide * rows)
            w = weight((me + first) * rows + across, me * rows + down)

            def body(h, at):
                scores = dot_nt(near(K, at), far(Q, first, at))
                pointwise(scores, w, far_col_probs.at[g, h], far_col_slope.at[g, h])

            each_head(1, body)

    def near_back(h, at):
        grad_probs = dot_nt(near(G, at), near(V, at))
        gq_sum[:, at] = dot_nn((grad_probs * row_slope[h]).astype(jnp.bfloat16), near(K, at))
        grad_probs = dot_nt(near(V, at), near(G, at))
        gk_sum[:, at] = dot_nn((grad_probs * col_slope[h]).astype(jnp.bfloat16), near(Q, at))
        gv_sum[:, at] = dot_nn(col_probs[h], near(G, at))

    each_head(2, near_back)
    for g in range(groups):
        first = 1 + g * wide

        @pl.when(me >= first)
        def _():
            def body(h, at):
                grad_probs = dot_nt(near(G, at), far(V, first, at))
                grad_scores = (grad_probs * far_row_slope[g, h]).astype(jnp.bfloat16)
                gq_sum[:, at] += dot_nn(grad_scores, far(K, first, at))

            each_head(1, body)

    results[2] = (gq_sum[...] * scale).astype(jnp.bfloat16)
    stores[2].start()

    arrive_all(G)
    @pl.loop(1, n)
    def _(j):
        src = lax.rem(me + j, n)
        pltpu.make_async_remote_copy(
            src_ref=part, dst_ref=seq_parts.at[src],
            send_sem=seq_send.at[j], recv_sem=seq_recv.at[src],
            device_id={"seq": src}, device_id_type=MESH,
        ).wait_recv()

    group = seq_parts[0]
    for j in range(1, n):
        group = group + seq_parts[j]
    total[...] = group
    pl.loop(1, m)(lambda j: own_share(j).start())
    own_parts[mine] = group

    for g in range(groups):
        first = 1 + g * wide

        @pl.when(me + first < n)
        def _():
            if not relayed:
                arrive_group(G, first)

            def body(h, at):
                back = far(G, first, at)
                grad_probs = dot_nt(near(V, at), back)
                grad_scores = (grad_probs * far_col_slope[g, h]).astype(jnp.bfloat16)
                gk_sum[:, at] += dot_nn(grad_scores, far(Q, first, at))
                gv_sum[:, at] += dot_nn(far_col_probs[g, h], back)

            each_head(1, body)

    results[3] = (gk_sum[...] * scale).astype(jnp.bfloat16)
    results[4] = gv_sum[...].astype(jnp.bfloat16)
    stores[3].start()
    stores[4].start()

    @pl.loop(1, m)
    def _(j):
        src = lax.rem(mine + j, m)
        pltpu.make_async_remote_copy(
            src_ref=total, dst_ref=own_parts.at[src],
            send_sem=own_send.at[j], recv_sem=own_recv.at[src],
            device_id={"own": src}, device_id_type=MESH,
        ).wait_recv()

    whole = own_parts[0]
    for j in range(1, m):
        whole = whole + own_parts[j]
    part_sum[...] = whole
    last = pltpu.make_async_copy(part_sum, ggain_hbm, store_sem.at[5])
    last.start()

    for what in (K, V, Q, G):
        wait_sends(what)
        if relayed:
            @pl.when(me == (3 if later(what) else 0))
            def _():
                for c in everything:
                    relay(what, c).wait_send()
    pl.loop(1, n)(lambda j: seq_share(j).wait_send())
    pl.loop(1, m)(lambda j: own_share(j).wait_send())
    for copy in stores + [last]:
        copy.wait()


def finish(*refs):
    sources, results, held, sem = refs[:6], refs[6:12], refs[12:18], refs[18]
    loads = [pltpu.make_async_copy(a, b, sem.at[0, i]) for i, (a, b) in enumerate(zip(sources, held))]
    stores = [pltpu.make_async_copy(a, b, sem.at[1, i]) for i, (a, b) in enumerate(zip(held, results))]
    for copy in loads:
        copy.start()
    for load, store in zip(loads, stores):
        load.wait()
        store.start()
    for copy in stores:
        copy.wait()


def per_device(n, m, queries, keys, values, gates, lengths, gain, grad_out):
    rows, width = queries.shape[1], queries.shape[2]
    head = width // H
    reach = min(n - 1, (rows * n // 2 - 1) // rows + 1)
    slots = reach + 1
    wide = 2 if reach % 2 == 0 else 1
    groups = reach // wide
    hbm = pl.BlockSpec(memory_space=pltpu.HBM)
    any_spec = pl.BlockSpec(memory_space=pl.ANY)
    block = jax.ShapeDtypeStruct(queries.shape, jnp.bfloat16)
    shapes = [block] * 5 + [jax.ShapeDtypeStruct((1, width), jnp.float32)]
    dma = pltpu.SemaphoreType.DMA
    outs = pl.pallas_call(
        functools.partial(kernel, n, m, reach, wide, 1.0 / math.sqrt(head)),
        out_shape=shapes,
        in_specs=[hbm] * 7,
        out_specs=[any_spec] * 6,
        scratch_shapes=[
            pltpu.SMEM(lengths.shape, jnp.int32),
            pltpu.VMEM((1, width), jnp.float32),
            pltpu.VMEM((4, slots, rows, width), jnp.bfloat16),
            pltpu.VMEM((rows, width), jnp.bfloat16),
            pltpu.VMEM((rows, width), jnp.bfloat16),
            pltpu.VMEM((H, rows, rows), jnp.bfloat16),
            pltpu.VMEM((H, rows, rows), jnp.float32),
            pltpu.VMEM((H, rows, rows), jnp.bfloat16),
            pltpu.VMEM((H, rows, rows), jnp.float32),
            pltpu.VMEM((groups, H, rows, wide * rows), jnp.bfloat16),
            pltpu.VMEM((groups, H, rows, wide * rows), jnp.float32),
            pltpu.VMEM((groups, H, rows, wide * rows), jnp.bfloat16),
            pltpu.VMEM((groups, H, rows, wide * rows), jnp.float32),
            pltpu.VMEM((rows, width), jnp.float32),
            pltpu.VMEM((rows, width), jnp.float32),
            pltpu.VMEM((rows, width), jnp.float32),
            pltpu.VMEM((rows, width), jnp.float32),
            pltpu.VMEM((5, rows, width), jnp.bfloat16),
            pltpu.VMEM((1, width), jnp.float32),
            pltpu.VMEM((n, 1, width), jnp.float32),
            pltpu.VMEM((1, width), jnp.float32),
            pltpu.VMEM((m, 1, width), jnp.float32),
            pltpu.VMEM((1, width), jnp.float32),
            dma((7,)), dma((6,)), dma((4, slots, PIECES)), dma((4, slots, PIECES)), dma((4, PIECES)),
            dma((n,)), dma((n,)), dma((m,)), dma((m,)),
        ],
        compiler_params=pltpu.CompilerParams(
            collective_id=0, has_side_effects=True, vmem_limit_bytes=ROOM
        ),
        cost_estimate=pl.CostEstimate(
            flops=16 * slots * rows * rows * width, bytes_accessed=20 * rows * width, transcendentals=0
        ),
    )(lengths, gain.reshape(1, width), queries, keys, values, gates, grad_out)
    output, grad_q, grad_k, grad_v, grad_gate, grad_gain = pl.pallas_call(
        finish,
        out_shape=shapes,
        in_specs=[any_spec] * 6,
        out_specs=[any_spec] * 6,
        scratch_shapes=[pltpu.VMEM(x.shape, x.dtype) for x in shapes] + [dma((2, 6))],
        compiler_params=pltpu.CompilerParams(has_side_effects=True, vmem_limit_bytes=ROOM),
    )(*outs)
    return output, grad_q, grad_k, grad_v, grad_gate, grad_gain.reshape(width)


def solution(mesh):
    blocked = P("own", "seq", None)
    sizes = (mesh.shape["seq"], mesh.shape["own"])
    return jax.shard_map(
        functools.partial(per_device, *sizes),
        mesh=mesh,
        in_specs=(blocked, blocked, blocked, blocked, P("own", None), P(), blocked),
        out_specs=(blocked, blocked, blocked, blocked, blocked, P()),
        check_vma=False,
    )
```

```python
import functools
import math

import jax
import jax.numpy as jnp
from jax import lax
from jax.experimental import pallas as pl
from jax.experimental.pallas import tpu as pltpu
from jax.sharding import PartitionSpec as P

H = 8
MESH = pl.DeviceIdType.MESH
K, V, Q, G = 0, 1, 2, 3
PIECES = 4
HALVES = 2
ROOM = 60 * 1024 * 1024


def dot_nt(a, b):
    return lax.dot_general(a, b, (((1,), (1,)), ((), ())), preferred_element_type=jnp.float32)


def dot_nn(a, b):
    return lax.dot_general(a, b, (((1,), (0,)), ((), ())), preferred_element_type=jnp.float32)


def silu_and_slope(scores):
    sig = 0.5 * jnp.tanh(0.5 * scores) + 0.5
    silu = scores * sig
    return silu, sig + silu * (1.0 - sig)


def kernel(
    n, m, reach, wide, scale,
    lens_hbm, gain_hbm, q_hbm, k_hbm, v_hbm, gate_hbm, grad_hbm,
    out_hbm, gq_hbm, gk_hbm, gv_hbm, gg_hbm, ggain_hbm,
    lens_ref, gain_ref, blocks, gate, grad,
    row_probs, row_slope, col_probs, col_slope,
    far_row_probs, far_row_slope, far_col_probs, far_col_slope,
    attended, gq_sum, gk_sum, gv_sum, results,
    part, seq_parts, total, own_parts, part_sum,
    load_sem, store_sem, send_sem, recv_sem, relay_sem, seq_send, seq_recv, own_send, own_recv,
):
    me = lax.axis_index("seq")
    mine = lax.axis_index("own")
    rows, width = gate.shape
    head = width // H
    users = lens_ref.shape[1]
    groups = reach // wide
    relayed = n == 4 and reach == 2
    piece = rows // PIECES
    everything = range(PIECES)

    def near(what, h):
        return blocks[what, 0, :, h]

    def far(what, first, h):
        return blocks[what, pl.ds(first, wide), :, h].reshape(wide * rows, head)

    def far_half(what, first, wide, half, h):
        length = rows // HALVES
        return blocks[what, pl.ds(first, wide), pl.ds(half * length, length), h].reshape(wide * length, head)

    def each_head(count, body):
        @pl.loop(0, H // count)
        def _(i):
            for j in range(count):
                h = i * count + j
                body(h, pl.ds(pl.multiple_of(h * head, head), head))

    def load(i, src, dst):
        return pltpu.make_async_copy(src, dst, load_sem.at[i])

    loads = [
        load(0, k_hbm.at[0], blocks.at[K, 0]),
        load(1, v_hbm.at[0], blocks.at[V, 0]),
        load(2, q_hbm.at[0], blocks.at[Q, 0]),
        load(3, gate_hbm.at[0], gate),
        load(4, grad_hbm.at[0], grad),
        load(5, gain_hbm, gain_ref),
        load(6, lens_hbm, lens_ref),
    ]
    for copy in loads:
        copy.start()

    barrier = pltpu.get_barrier_semaphore()

    @pl.loop(1, n)
    def _(j):
        pl.semaphore_signal(barrier, 1, device_id={"seq": lax.rem(me + j, n)}, device_id_type=MESH)

    @pl.loop(1, m)
    def _(j):
        pl.semaphore_signal(barrier, 1, device_id={"own": lax.rem(mine + j, m)}, device_id_type=MESH)

    for copy in loads[:3]:
        copy.wait()
    pl.semaphore_wait(barrier, n + m - 2)

    def later(what):
        return what in (K, V)

    def span(c):
        return pl.ds(c * piece if isinstance(c, int) else pl.multiple_of(c * piece, piece), piece)

    def send(what, d, c):
        return pltpu.make_async_remote_copy(
            src_ref=blocks.at[what, 0, span(c)], dst_ref=blocks.at[what, d, span(c)],
            send_sem=send_sem.at[what, d, c], recv_sem=recv_sem.at[what, d, c],
            device_id={"seq": me + d if later(what) else me - d}, device_id_type=MESH,
        )

    def relay(what, c):
        return pltpu.make_async_remote_copy(
            src_ref=blocks.at[what, 2, span(c)], dst_ref=blocks.at[what, 1, span(c)],
            send_sem=relay_sem.at[what, c], recv_sem=recv_sem.at[what, 1, c],
            device_id={"seq": 2 if later(what) else 1}, device_id_type=MESH,
        )

    def can_send(what, d):
        ok = me + d < n if later(what) else me >= d
        if relayed and d == 1:
            ok = ok & (me != (1 if later(what) else 2))
        return ok

    def start(what, pieces):
        for d in range(1, reach + 1):
            @pl.when(can_send(what, d))
            def _():
                for c in pieces:
                    send(what, d, c).start()

    def wait_sends(what):
        for d in range(1, reach + 1):
            @pl.when(can_send(what, d))
            def _():
                for c in everything:
                    send(what, d, c).wait_send()

    def arrive(what, d, pieces=everything):
        for c in pieces:
            send(what, d, c).wait_recv()

    def arrive_and_relay(what, pieces=everything):
        for c in pieces:
            send(what, 2, c).wait_recv()
            relay(what, c).start()

    def arrive_group(what, first, pieces=everything):
        for d in range(first, first + wide):
            pl.when(me >= d if later(what) else me + d < n)(functools.partial(arrive, what, d, pieces))

    def arrive_all(what, pieces=everything):
        if relayed:
            relayer = 3 if later(what) else 0

            @pl.when(me == relayer)
            def _():
                arrive_and_relay(what, pieces)
                arrive(what, 1, pieces)

            pl.when(me != relayer)(functools.partial(arrive_group, what, 1, pieces))

    start(K, everything)
    start(V, everything)
    if relayed:
        pl.when(me != 3)(functools.partial(start, Q, everything))

        @pl.when(me == 3)
        def _():
            for c in everything:
                send(Q, 2, c).start()
            for c in everything[: PIECES // 2]:
                send(Q, 1, c).start()
    else:
        start(Q, everything)

    if wide == 2:
        for d in range(2, reach + 1, 2):
            @pl.when(me == d - 1)
            def _():
                blocks[K, d] = jnp.zeros((rows, width), jnp.bfloat16)
                blocks[V, d] = jnp.zeros((rows, width), jnp.bfloat16)

    def weight(t, s):
        first = jnp.zeros_like(t)
        length = jnp.ones_like(t)
        end = jnp.int32(0)
        for u in range(users):
            begin, end = end, end + lens_ref[0, u]
            inside = (t >= begin) & (t < end)
            first = jnp.where(inside, begin, first)
            length = jnp.where(inside, lens_ref[0, u], length)
        return jnp.where((s >= first) & (s <= t), 1.0 / length.astype(jnp.float32), 0.0)

    def iotas(columns):
        return [lax.broadcasted_iota(jnp.int32, (rows, columns), i) for i in (0, 1)]

    for copy in loads[5:]:
        copy.wait()

    def pointwise(scores, w, probs_ref, slope_ref):
        scores = scores * scale
        silu, slope = silu_and_slope(scores)
        probs = (silu * w).astype(jnp.bfloat16)
        probs_ref[...] = probs
        slope_ref[...] = slope * w
        return probs

    down, across = iotas(rows)
    w = weight(me * rows + down, me * rows + across)

    def near_forward(h, at):
        probs = pointwise(dot_nt(near(Q, at), near(K, at)), w, row_probs.at[h], row_slope.at[h])
        attended[:, at] = dot_nn(probs, near(V, at))

    each_head(4, near_forward)

    near_w = weight(me * rows + across, me * rows + down)

    def near_column(h, at):
        pointwise(dot_nt(near(K, at), near(Q, at)), near_w, col_probs.at[h], col_slope.at[h])

    each_head(4, near_column)

    arrive_all(K)
    for g in range(groups):
        first = 1 + g * wide

        @pl.when(me >= first)
        def _():
            if not relayed:
                arrive_group(K, first)
            down, across = iotas(wide * rows)
            s = (me - first) * rows + across - jnp.where(across >= rows, 2 * rows, 0)
            w = weight(me * rows + down, s)

            def body(h, at):
                scores = dot_nt(near(Q, at), far(K, first, at))
                pointwise(scores, w, far_row_probs.at[g, h], far_row_slope.at[g, h])

            each_head(4, body)

    arrive_all(V)
    if relayed:
        @pl.when(me == 3)
        def _():
            for c in everything[PIECES // 2 :]:
                send(Q, 1, c).start()
    for g in range(groups):
        first = 1 + g * wide

        @pl.when(me >= first)
        def _():
            if not relayed:
                arrive_group(V, first)

            def body(h, at):
                attended[:, at] += dot_nn(far_row_probs[g, h], far(V, first, at))

            each_head(4, body)

    for copy in loads[3:5]:
        copy.wait()
    gain = gain_ref[...]
    step = piece

    @pl.loop(0, HALVES)
    def _(half):
        pieces = [half * (PIECES // HALVES) + c for c in range(PIECES // HALVES)]
        for c in pieces:
            at = span(c)
            att = attended[at, :]
            center = att - jnp.mean(att, axis=1, keepdims=True)
            rstd = lax.rsqrt(jnp.mean(center * center, axis=1, keepdims=True) + 1e-05)
            normed = center * rstd
            dnorm = grad[at, :].astype(jnp.float32) * gate[at, :].astype(jnp.float32) * gain
            back = rstd * (
                dnorm
                - jnp.mean(dnorm, axis=1, keepdims=True)
                - normed * jnp.mean(dnorm * normed, axis=1, keepdims=True)
            )
            attended[at, :] = normed
            blocks[G, 0, at, :] = back.astype(jnp.bfloat16)
        start(G, pieces)

    part[...] = jnp.zeros((1, width), jnp.float32)

    @pl.loop(0, rows // step)
    def _(i):
        at = pl.ds(pl.multiple_of(i * step, step), step)
        normed = attended[at, :]
        gate_f = gate[at, :].astype(jnp.float32)
        grad_f = grad[at, :].astype(jnp.float32)
        results[0, at, :] = (normed * gain * gate_f).astype(jnp.bfloat16)
        results[1, at, :] = (grad_f * normed * gain).astype(jnp.bfloat16)
        part[...] += jnp.sum(grad_f * gate_f * normed, axis=0, keepdims=True)

    def seq_share(j):
        return pltpu.make_async_remote_copy(
            src_ref=part, dst_ref=seq_parts.at[me],
            send_sem=seq_send.at[j], recv_sem=seq_recv.at[me],
            device_id={"seq": lax.rem(me + j, n)}, device_id_type=MESH,
        )

    def own_share(j):
        return pltpu.make_async_remote_copy(
            src_ref=total, dst_ref=own_parts.at[mine],
            send_sem=own_send.at[j], recv_sem=own_recv.at[mine],
            device_id={"own": lax.rem(mine + j, m)}, device_id_type=MESH,
        )

    pl.loop(1, n)(lambda j: seq_share(j).start())
    seq_parts[me] = part[...]

    def store(i, dst):
        return pltpu.make_async_copy(results.at[i], dst.at[0], store_sem.at[i])

    stores = [store(i, dst) for i, dst in enumerate((out_hbm, gg_hbm, gq_hbm, gk_hbm, gv_hbm))]
    stores[0].start()
    stores[1].start()

    def near_back(h, at):
        grad_probs = dot_nt(near(G, at), near(V, at))
        gq_sum[:, at] = dot_nn((grad_probs * row_slope[h]).astype(jnp.bfloat16), near(K, at))
        grad_probs = dot_nt(near(V, at), near(G, at))
        gk_sum[:, at] = dot_nn((grad_probs * col_slope[h]).astype(jnp.bfloat16), near(Q, at))
        gv_sum[:, at] = dot_nn(col_probs[h], near(G, at))

    each_head(4, near_back)
    for g in range(groups):
        first = 1 + g * wide

        @pl.when(me >= first)
        def _():
            def body(h, at):
                grad_probs = dot_nt(near(G, at), far(V, first, at))
                grad_scores = (grad_probs * far_row_slope[g, h]).astype(jnp.bfloat16)
                gq_sum[:, at] += dot_nn(grad_scores, far(K, first, at))

            each_head(4, body)

    results[2] = (gq_sum[...] * scale).astype(jnp.bfloat16)
    stores[2].start()

    def columns(first, body):
        if wide == 2:
            pl.when(me + first + 1 < n)(functools.partial(body, 2))
            pl.when(me + first + 1 == n)(functools.partial(body, 1))
        else:
            pl.when(me + first < n)(functools.partial(body, 1))

    def far_column(g, first, slots):
        count = slots * rows // HALVES
        down, across = iotas(count)
        lanes = pl.ds(0, count)
        for half in range(HALVES):
            t = (me + first) * rows + half * (rows // HALVES) + across
            if slots == 2:
                t = t + jnp.where(across >= rows // HALVES, rows - rows // HALVES, 0)
            w = weight(t, me * rows + down)

            def body(h, at):
                scores = dot_nt(near(K, at), far_half(Q, first, slots, half, at))
                pointwise(scores, w, far_col_probs.at[g, half, h, :, lanes], far_col_slope.at[g, half, h, :, lanes])

            each_head(4, body)

    def far_column_back(g, first, half, slots):
        lanes = pl.ds(0, slots * rows // HALVES)

        def body(h, at):
            back = far_half(G, first, slots, half, at)
            grad_probs = dot_nt(near(V, at), back)
            grad_scores = (grad_probs * far_col_slope[g, half, h, :, lanes]).astype(jnp.bfloat16)
            gk_sum[:, at] += dot_nn(grad_scores, far_half(Q, first, slots, half, at))
            gv_sum[:, at] += dot_nn(far_col_probs[g, half, h, :, lanes], back)

        each_head(4, body)

    def sum_over_seq():
        @pl.loop(1, n)
        def _(j):
            src = lax.rem(me + j, n)
            pltpu.make_async_remote_copy(
                src_ref=part, dst_ref=seq_parts.at[src],
                send_sem=seq_send.at[j], recv_sem=seq_recv.at[src],
                device_id={"seq": src}, device_id_type=MESH,
            ).wait_recv()

        group = seq_parts[0]
        for j in range(1, n):
            group = group + seq_parts[j]
        total[...] = group
        pl.loop(1, m)(lambda j: own_share(j).start())
        own_parts[mine] = group

    arrive_all(Q)
    for g in range(groups):
        first = 1 + g * wide
        if not relayed:
            arrive_group(Q, first)
        columns(first, functools.partial(far_column, g, first))

    for half in range(HALVES):
        pieces = everything[half * PIECES // HALVES : (half + 1) * PIECES // HALVES]
        arrive_all(G, pieces)
        if half == HALVES - 1:
            sum_over_seq()
        for g in range(groups):
            first = 1 + g * wide
            if not relayed:
                arrive_group(G, first, pieces)
            columns(first, functools.partial(far_column_back, g, first, half))

    results[3] = (gk_sum[...] * scale).astype(jnp.bfloat16)
    results[4] = gv_sum[...].astype(jnp.bfloat16)
    stores[3].start()
    stores[4].start()

    @pl.loop(1, m)
    def _(j):
        src = lax.rem(mine + j, m)
        pltpu.make_async_remote_copy(
            src_ref=total, dst_ref=own_parts.at[src],
            send_sem=own_send.at[j], recv_sem=own_recv.at[src],
            device_id={"own": src}, device_id_type=MESH,
        ).wait_recv()

    whole = own_parts[0]
    for j in range(1, m):
        whole = whole + own_parts[j]
    part_sum[...] = whole
    last = pltpu.make_async_copy(part_sum, ggain_hbm, store_sem.at[5])
    last.start()

    for what in (K, V, Q, G):
        wait_sends(what)
        if relayed:
            @pl.when(me == (3 if later(what) else 0))
            def _():
                for c in everything:
                    relay(what, c).wait_send()
    pl.loop(1, n)(lambda j: seq_share(j).wait_send())
    pl.loop(1, m)(lambda j: own_share(j).wait_send())
    for copy in stores + [last]:
        copy.wait()


def finish(*refs):
    sources, results, held, sem = refs[:6], refs[6:12], refs[12:18], refs[18]
    loads = [pltpu.make_async_copy(a, b, sem.at[0, i]) for i, (a, b) in enumerate(zip(sources, held))]
    stores = [pltpu.make_async_copy(a, b, sem.at[1, i]) for i, (a, b) in enumerate(zip(held, results))]
    for copy in loads:
        copy.start()
    for load, store in zip(loads, stores):
        load.wait()
        store.start()
    for copy in stores:
        copy.wait()


def per_device(n, m, queries, keys, values, gates, lengths, gain, grad_out):
    rows, width = queries.shape[1], queries.shape[2]
    head = width // H
    reach = min(n - 1, (rows * n // 2 - 1) // rows + 1)
    slots = reach + 1
    wide = 2 if reach % 2 == 0 else 1
    groups = reach // wide
    hbm = pl.BlockSpec(memory_space=pltpu.HBM)
    any_spec = pl.BlockSpec(memory_space=pl.ANY)
    block = jax.ShapeDtypeStruct(queries.shape, jnp.bfloat16)
    shapes = [block] * 5 + [jax.ShapeDtypeStruct((1, width), jnp.float32)]
    dma = pltpu.SemaphoreType.DMA
    outs = pl.pallas_call(
        functools.partial(kernel, n, m, reach, wide, 1.0 / math.sqrt(head)),
        out_shape=shapes,
        in_specs=[hbm] * 7,
        out_specs=[any_spec] * 6,
        scratch_shapes=[
            pltpu.SMEM(lengths.shape, jnp.int32),
            pltpu.VMEM((1, width), jnp.float32),
            pltpu.VMEM((4, slots, rows, width), jnp.bfloat16),
            pltpu.VMEM((rows, width), jnp.bfloat16),
            pltpu.VMEM((rows, width), jnp.bfloat16),
            pltpu.VMEM((H, rows, rows), jnp.bfloat16),
            pltpu.VMEM((H, rows, rows), jnp.float32),
            pltpu.VMEM((H, rows, rows), jnp.bfloat16),
            pltpu.VMEM((H, rows, rows), jnp.float32),
            pltpu.VMEM((groups, H, rows, wide * rows), jnp.bfloat16),
            pltpu.VMEM((groups, H, rows, wide * rows), jnp.float32),
            pltpu.VMEM((groups, HALVES, H, rows, wide * rows // HALVES), jnp.bfloat16),
            pltpu.VMEM((groups, HALVES, H, rows, wide * rows // HALVES), jnp.float32),
            pltpu.VMEM((rows, width), jnp.float32),
            pltpu.VMEM((rows, width), jnp.float32),
            pltpu.VMEM((rows, width), jnp.float32),
            pltpu.VMEM((rows, width), jnp.float32),
            pltpu.VMEM((5, rows, width), jnp.bfloat16),
            pltpu.VMEM((1, width), jnp.float32),
            pltpu.VMEM((n, 1, width), jnp.float32),
            pltpu.VMEM((1, width), jnp.float32),
            pltpu.VMEM((m, 1, width), jnp.float32),
            pltpu.VMEM((1, width), jnp.float32),
            dma((7,)), dma((6,)), dma((4, slots, PIECES)), dma((4, slots, PIECES)), dma((4, PIECES)),
            dma((n,)), dma((n,)), dma((m,)), dma((m,)),
        ],
        compiler_params=pltpu.CompilerParams(
            collective_id=0, has_side_effects=True, vmem_limit_bytes=ROOM
        ),
        cost_estimate=pl.CostEstimate(
            flops=16 * slots * rows * rows * width, bytes_accessed=20 * rows * width, transcendentals=0
        ),
    )(lengths, gain.reshape(1, width), queries, keys, values, gates, grad_out)
    output, grad_q, grad_k, grad_v, grad_gate, grad_gain = pl.pallas_call(
        finish,
        out_shape=shapes,
        in_specs=[any_spec] * 6,
        out_specs=[any_spec] * 6,
        scratch_shapes=[pltpu.VMEM(x.shape, x.dtype) for x in shapes] + [dma((2, 6))],
        compiler_params=pltpu.CompilerParams(has_side_effects=True, vmem_limit_bytes=ROOM),
    )(*outs)
    return output, grad_q, grad_k, grad_v, grad_gate, grad_gain.reshape(width)


def solution(mesh):
    blocked = P("own", "seq", None)
    sizes = (mesh.shape["seq"], mesh.shape["own"])
    return jax.shard_map(
        functools.partial(per_device, *sizes),
        mesh=mesh,
        in_specs=(blocked, blocked, blocked, blocked, P("own", None), P(), blocked),
        out_specs=(blocked, blocked, blocked, blocked, blocked, P()),
        check_vma=False,
    )
```

```python
import functools
import math

import jax
import jax.numpy as jnp
from jax import lax
from jax.experimental import pallas as pl
from jax.experimental.pallas import tpu as pltpu
from jax.sharding import PartitionSpec as P

H = 8
MESH = pl.DeviceIdType.MESH
K, V, Q, G = 0, 1, 2, 3
PIECES = 4
HALVES = 2
ROOM = 60 * 1024 * 1024


def dot_nt(a, b):
    return lax.dot_general(a, b, (((1,), (1,)), ((), ())), preferred_element_type=jnp.float32)


def dot_nn(a, b):
    return lax.dot_general(a, b, (((1,), (0,)), ((), ())), preferred_element_type=jnp.float32)


def silu_and_slope(scores):
    sig = 0.5 * jnp.tanh(0.5 * scores) + 0.5
    silu = scores * sig
    return silu, sig + silu * (1.0 - sig)


def kernel(
    n, m, reach, wide, scale,
    lens_hbm, gain_hbm, q_hbm, k_hbm, v_hbm, gate_hbm, grad_hbm,
    out_hbm, gq_hbm, gk_hbm, gv_hbm, gg_hbm, ggain_hbm,
    lens_ref, gain_ref, blocks, gate, grad,
    row_probs, row_slope, col_probs, col_slope,
    far_row_probs, far_row_slope, far_col_probs, far_col_slope,
    attended, gq_sum, gk_sum, gv_sum, results,
    part, seq_parts, total, own_parts, part_sum,
    load_sem, store_sem, send_sem, recv_sem, relay_sem, seq_send, seq_recv, own_send, own_recv,
):
    me = lax.axis_index("seq")
    mine = lax.axis_index("own")
    rows, width = gate.shape
    head = width // H
    users = lens_ref.shape[1]
    groups = reach // wide
    relayed = n == 4 and reach == 2
    piece = rows // PIECES
    everything = range(PIECES)

    def near(what, h):
        return blocks[what, 0, :, h]

    def far(what, first, h):
        return blocks[what, pl.ds(first, wide), :, h].reshape(wide * rows, head)

    def far_half(what, first, wide, half, h):
        length = rows // HALVES
        return blocks[what, pl.ds(first, wide), pl.ds(half * length, length), h].reshape(wide * length, head)

    def each_head(count, body):
        @pl.loop(0, H // count)
        def _(i):
            for j in range(count):
                h = i * count + j
                body(h, pl.ds(pl.multiple_of(h * head, head), head))

    def load(i, src, dst):
        return pltpu.make_async_copy(src, dst, load_sem.at[i])

    loads = [
        load(0, k_hbm.at[0], blocks.at[K, 0]),
        load(1, v_hbm.at[0], blocks.at[V, 0]),
        load(2, q_hbm.at[0], blocks.at[Q, 0]),
        load(3, gate_hbm.at[0], gate),
        load(4, grad_hbm.at[0], grad),
        load(5, gain_hbm, gain_ref),
        load(6, lens_hbm, lens_ref),
    ]
    for copy in loads:
        copy.start()

    barrier = pltpu.get_barrier_semaphore()

    @pl.loop(1, n)
    def _(j):
        pl.semaphore_signal(barrier, 1, device_id={"seq": lax.rem(me + j, n)}, device_id_type=MESH)

    @pl.loop(1, m)
    def _(j):
        pl.semaphore_signal(barrier, 1, device_id={"own": lax.rem(mine + j, m)}, device_id_type=MESH)

    for copy in loads[:3]:
        copy.wait()
    pl.semaphore_wait(barrier, n + m - 2)

    def later(what):
        return what in (K, V)

    def span(c):
        return pl.ds(c * piece if isinstance(c, int) else pl.multiple_of(c * piece, piece), piece)

    def send(what, d, c):
        return pltpu.make_async_remote_copy(
            src_ref=blocks.at[what, 0, span(c)], dst_ref=blocks.at[what, d, span(c)],
            send_sem=send_sem.at[what, d, c], recv_sem=recv_sem.at[what, d, c],
            device_id={"seq": me + d if later(what) else me - d}, device_id_type=MESH,
        )

    def relay(what, c):
        return pltpu.make_async_remote_copy(
            src_ref=blocks.at[what, 2, span(c)], dst_ref=blocks.at[what, 1, span(c)],
            send_sem=relay_sem.at[what, c], recv_sem=recv_sem.at[what, 1, c],
            device_id={"seq": 2 if later(what) else 1}, device_id_type=MESH,
        )

    def can_send(what, d):
        ok = me + d < n if later(what) else me >= d
        if relayed and d == 1:
            ok = ok & (me != (1 if later(what) else 2))
        return ok

    def start(what, pieces):
        for d in range(1, reach + 1):
            @pl.when(can_send(what, d))
            def _():
                for c in pieces:
                    send(what, d, c).start()

    def wait_sends(what):
        for d in range(1, reach + 1):
            @pl.when(can_send(what, d))
            def _():
                for c in everything:
                    send(what, d, c).wait_send()

    def arrive(what, d, pieces=everything):
        for c in pieces:
            send(what, d, c).wait_recv()

    def arrive_and_relay(what, pieces=everything):
        for c in pieces:
            send(what, 2, c).wait_recv()
            relay(what, c).start()

    def arrive_group(what, first, pieces=everything):
        for d in range(first, first + wide):
            pl.when(me >= d if later(what) else me + d < n)(functools.partial(arrive, what, d, pieces))

    def arrive_all(what, pieces=everything):
        if relayed:
            relayer = 3 if later(what) else 0

            @pl.when(me == relayer)
            def _():
                arrive_and_relay(what, pieces)
                arrive(what, 1, pieces)

            pl.when(me != relayer)(functools.partial(arrive_group, what, 1, pieces))

    start(K, everything)
    if relayed:
        @pl.when(me == 3)
        def _():
            for c in everything:
                send(Q, 2, c).start()
            for c in everything[: PIECES // 2]:
                send(Q, 1, c).start()

    if wide == 2:
        for d in range(2, reach + 1, 2):
            @pl.when(me == d - 1)
            def _():
                blocks[K, d] = jnp.zeros((rows, width), jnp.bfloat16)
                blocks[V, d] = jnp.zeros((rows, width), jnp.bfloat16)

    def weight(t, s):
        first = jnp.zeros_like(t)
        length = jnp.ones_like(t)
        end = jnp.int32(0)
        for u in range(users):
            begin, end = end, end + lens_ref[0, u]
            inside = (t >= begin) & (t < end)
            first = jnp.where(inside, begin, first)
            length = jnp.where(inside, lens_ref[0, u], length)
        return jnp.where((s >= first) & (s <= t), 1.0 / length.astype(jnp.float32), 0.0)

    def iotas(columns):
        return [lax.broadcasted_iota(jnp.int32, (rows, columns), i) for i in (0, 1)]

    for copy in loads[5:]:
        copy.wait()

    def pointwise(scores, w, probs_ref, slope_ref):
        scores = scores * scale
        silu, slope = silu_and_slope(scores)
        probs = (silu * w).astype(jnp.bfloat16)
        probs_ref[...] = probs
        slope_ref[...] = slope * w
        return probs

    down, across = iotas(rows)
    w = weight(me * rows + down, me * rows + across)

    def near_forward(h, at):
        probs = pointwise(dot_nt(near(Q, at), near(K, at)), w, row_probs.at[h], row_slope.at[h])
        attended[:, at] = dot_nn(probs, near(V, at))

    each_head(4, near_forward)

    near_w = weight(me * rows + across, me * rows + down)

    def near_column(h, at):
        pointwise(dot_nt(near(K, at), near(Q, at)), near_w, col_probs.at[h], col_slope.at[h])

    each_head(4, near_column)

    wait_sends(K)
    start(V, everything)
    if relayed:
        pl.when(me != 3)(functools.partial(start, Q, everything))
    else:
        start(Q, everything)

    arrive_all(K)
    for g in range(groups):
        first = 1 + g * wide

        @pl.when(me >= first)
        def _():
            if not relayed:
                arrive_group(K, first)
            down, across = iotas(wide * rows)
            s = (me - first) * rows + across - jnp.where(across >= rows, 2 * rows, 0)
            w = weight(me * rows + down, s)

            def body(h, at):
                scores = dot_nt(near(Q, at), far(K, first, at))
                pointwise(scores, w, far_row_probs.at[g, h], far_row_slope.at[g, h])

            each_head(4, body)

    arrive_all(V)
    if relayed:
        @pl.when(me == 3)
        def _():
            for c in everything[PIECES // 2 :]:
                send(Q, 1, c).start()
    if not relayed:
        for g in range(groups):
            arrive_group(V, 1 + g * wide)

    for copy in loads[3:5]:
        copy.wait()
    gain = gain_ref[...]
    step = piece

    @pl.loop(0, HALVES)
    def _(half):
        length = rows // HALVES
        part_rows = pl.ds(pl.multiple_of(half * length, length), length)
        for g in range(groups):
            first = 1 + g * wide

            @pl.when(me >= first)
            def _():
                def body(h, at):
                    attended[part_rows, at] += dot_nn(far_row_probs[g, h, part_rows, :], far(V, first, at))

                each_head(H, body)

        pieces = [half * (PIECES // HALVES) + c for c in range(PIECES // HALVES)]
        for c in pieces:
            at = span(c)
            att = attended[at, :]
            center = att - jnp.mean(att, axis=1, keepdims=True)
            rstd = lax.rsqrt(jnp.mean(center * center, axis=1, keepdims=True) + 1e-05)
            normed = center * rstd
            dnorm = grad[at, :].astype(jnp.float32) * gate[at, :].astype(jnp.float32) * gain
            back = rstd * (
                dnorm
                - jnp.mean(dnorm, axis=1, keepdims=True)
                - normed * jnp.mean(dnorm * normed, axis=1, keepdims=True)
            )
            attended[at, :] = normed
            blocks[G, 0, at, :] = back.astype(jnp.bfloat16)
        start(G, pieces)

    part[...] = jnp.zeros((1, width), jnp.float32)

    @pl.loop(0, rows // step)
    def _(i):
        at = pl.ds(pl.multiple_of(i * step, step), step)
        normed = attended[at, :]
        gate_f = gate[at, :].astype(jnp.float32)
        grad_f = grad[at, :].astype(jnp.float32)
        results[0, at, :] = (normed * gain * gate_f).astype(jnp.bfloat16)
        results[1, at, :] = (grad_f * normed * gain).astype(jnp.bfloat16)
        part[...] += jnp.sum(grad_f * gate_f * normed, axis=0, keepdims=True)

    def seq_share(j):
        return pltpu.make_async_remote_copy(
            src_ref=part, dst_ref=seq_parts.at[me],
            send_sem=seq_send.at[j], recv_sem=seq_recv.at[me],
            device_id={"seq": lax.rem(me + j, n)}, device_id_type=MESH,
        )

    def own_share(j):
        return pltpu.make_async_remote_copy(
            src_ref=total, dst_ref=own_parts.at[mine],
            send_sem=own_send.at[j], recv_sem=own_recv.at[mine],
            device_id={"own": lax.rem(mine + j, m)}, device_id_type=MESH,
        )

    pl.loop(1, n)(lambda j: seq_share(j).start())
    seq_parts[me] = part[...]

    def store(i, dst):
        return pltpu.make_async_copy(results.at[i], dst.at[0], store_sem.at[i])

    stores = [store(i, dst) for i, dst in enumerate((out_hbm, gg_hbm, gq_hbm, gk_hbm, gv_hbm))]
    stores[0].start()
    stores[1].start()

    def near_back(h, at):
        grad_probs = dot_nt(near(G, at), near(V, at))
        gq_sum[:, at] = dot_nn((grad_probs * row_slope[h]).astype(jnp.bfloat16), near(K, at))
        grad_probs = dot_nt(near(V, at), near(G, at))
        gk_sum[:, at] = dot_nn((grad_probs * col_slope[h]).astype(jnp.bfloat16), near(Q, at))
        gv_sum[:, at] = dot_nn(col_probs[h], near(G, at))

    each_head(4, near_back)
    for g in range(groups):
        first = 1 + g * wide

        @pl.when(me >= first)
        def _():
            def body(h, at):
                grad_probs = dot_nt(near(G, at), far(V, first, at))
                grad_scores = (grad_probs * far_row_slope[g, h]).astype(jnp.bfloat16)
                gq_sum[:, at] += dot_nn(grad_scores, far(K, first, at))

            each_head(4, body)

    results[2] = (gq_sum[...] * scale).astype(jnp.bfloat16)
    stores[2].start()

    def columns(first, body):
        if wide == 2:
            pl.when(me + first + 1 < n)(functools.partial(body, 2))
            pl.when(me + first + 1 == n)(functools.partial(body, 1))
        else:
            pl.when(me + first < n)(functools.partial(body, 1))

    def far_column(g, first, slots):
        count = slots * rows // HALVES
        down, across = iotas(count)
        lanes = pl.ds(0, count)
        for half in range(HALVES):
            t = (me + first) * rows + half * (rows // HALVES) + across
            if slots == 2:
                t = t + jnp.where(across >= rows // HALVES, rows - rows // HALVES, 0)
            w = weight(t, me * rows + down)

            def body(h, at):
                scores = dot_nt(near(K, at), far_half(Q, first, slots, half, at))
                pointwise(scores, w, far_col_probs.at[g, half, h, :, lanes], far_col_slope.at[g, half, h, :, lanes])

            each_head(4, body)

    def far_column_back(g, first, half, slots):
        lanes = pl.ds(0, slots * rows // HALVES)

        def body(h, at):
            back = far_half(G, first, slots, half, at)
            grad_probs = dot_nt(near(V, at), back)
            grad_scores = (grad_probs * far_col_slope[g, half, h, :, lanes]).astype(jnp.bfloat16)
            gk_sum[:, at] += dot_nn(grad_scores, far_half(Q, first, slots, half, at))
            gv_sum[:, at] += dot_nn(far_col_probs[g, half, h, :, lanes], back)

        each_head(4, body)

    def sum_over_seq():
        @pl.loop(1, n)
        def _(j):
            src = lax.rem(me + j, n)
            pltpu.make_async_remote_copy(
                src_ref=part, dst_ref=seq_parts.at[src],
                send_sem=seq_send.at[j], recv_sem=seq_recv.at[src],
                device_id={"seq": src}, device_id_type=MESH,
            ).wait_recv()

        group = seq_parts[0]
        for j in range(1, n):
            group = group + seq_parts[j]
        total[...] = group
        pl.loop(1, m)(lambda j: own_share(j).start())
        own_parts[mine] = group

    arrive_all(Q)
    for g in range(groups):
        first = 1 + g * wide
        if not relayed:
            arrive_group(Q, first)
        columns(first, functools.partial(far_column, g, first))

    for half in range(HALVES):
        pieces = everything[half * PIECES // HALVES : (half + 1) * PIECES // HALVES]
        arrive_all(G, pieces)
        if half == HALVES - 1:
            sum_over_seq()
        for g in range(groups):
            first = 1 + g * wide
            if not relayed:
                arrive_group(G, first, pieces)
            columns(first, functools.partial(far_column_back, g, first, half))

    results[3] = (gk_sum[...] * scale).astype(jnp.bfloat16)
    results[4] = gv_sum[...].astype(jnp.bfloat16)
    stores[3].start()
    stores[4].start()

    @pl.loop(1, m)
    def _(j):
        src = lax.rem(mine + j, m)
        pltpu.make_async_remote_copy(
            src_ref=total, dst_ref=own_parts.at[src],
            send_sem=own_send.at[j], recv_sem=own_recv.at[src],
            device_id={"own": src}, device_id_type=MESH,
        ).wait_recv()

    whole = own_parts[0]
    for j in range(1, m):
        whole = whole + own_parts[j]
    part_sum[...] = whole
    last = pltpu.make_async_copy(part_sum, ggain_hbm, store_sem.at[5])
    last.start()

    for what in (K, V, Q, G):
        if what != K:
            wait_sends(what)
        if relayed:
            @pl.when(me == (3 if later(what) else 0))
            def _():
                for c in everything:
                    relay(what, c).wait_send()
    pl.loop(1, n)(lambda j: seq_share(j).wait_send())
    pl.loop(1, m)(lambda j: own_share(j).wait_send())
    for copy in stores + [last]:
        copy.wait()


def finish(*refs):
    sources, results, held, sem = refs[:6], refs[6:12], refs[12:18], refs[18]
    loads = [pltpu.make_async_copy(a, b, sem.at[0, i]) for i, (a, b) in enumerate(zip(sources, held))]
    stores = [pltpu.make_async_copy(a, b, sem.at[1, i]) for i, (a, b) in enumerate(zip(held, results))]
    for copy in loads:
        copy.start()
    for load, store in zip(loads, stores):
        load.wait()
        store.start()
    for copy in stores:
        copy.wait()


def per_device(n, m, queries, keys, values, gates, lengths, gain, grad_out):
    rows, width = queries.shape[1], queries.shape[2]
    head = width // H
    reach = min(n - 1, (rows * n // 2 - 1) // rows + 1)
    slots = reach + 1
    wide = 2 if reach % 2 == 0 else 1
    groups = reach // wide
    hbm = pl.BlockSpec(memory_space=pltpu.HBM)
    any_spec = pl.BlockSpec(memory_space=pl.ANY)
    block = jax.ShapeDtypeStruct(queries.shape, jnp.bfloat16)
    shapes = [block] * 5 + [jax.ShapeDtypeStruct((1, width), jnp.float32)]
    dma = pltpu.SemaphoreType.DMA
    outs = pl.pallas_call(
        functools.partial(kernel, n, m, reach, wide, 1.0 / math.sqrt(head)),
        out_shape=shapes,
        in_specs=[hbm] * 7,
        out_specs=[any_spec] * 6,
        scratch_shapes=[
            pltpu.SMEM(lengths.shape, jnp.int32),
            pltpu.VMEM((1, width), jnp.float32),
            pltpu.VMEM((4, slots, rows, width), jnp.bfloat16),
            pltpu.VMEM((rows, width), jnp.bfloat16),
            pltpu.VMEM((rows, width), jnp.bfloat16),
            pltpu.VMEM((H, rows, rows), jnp.bfloat16),
            pltpu.VMEM((H, rows, rows), jnp.float32),
            pltpu.VMEM((H, rows, rows), jnp.bfloat16),
            pltpu.VMEM((H, rows, rows), jnp.float32),
            pltpu.VMEM((groups, H, rows, wide * rows), jnp.bfloat16),
            pltpu.VMEM((groups, H, rows, wide * rows), jnp.float32),
            pltpu.VMEM((groups, HALVES, H, rows, wide * rows // HALVES), jnp.bfloat16),
            pltpu.VMEM((groups, HALVES, H, rows, wide * rows // HALVES), jnp.float32),
            pltpu.VMEM((rows, width), jnp.float32),
            pltpu.VMEM((rows, width), jnp.float32),
            pltpu.VMEM((rows, width), jnp.float32),
            pltpu.VMEM((rows, width), jnp.float32),
            pltpu.VMEM((5, rows, width), jnp.bfloat16),
            pltpu.VMEM((1, width), jnp.float32),
            pltpu.VMEM((n, 1, width), jnp.float32),
            pltpu.VMEM((1, width), jnp.float32),
            pltpu.VMEM((m, 1, width), jnp.float32),
            pltpu.VMEM((1, width), jnp.float32),
            dma((7,)), dma((6,)), dma((4, slots, PIECES)), dma((4, slots, PIECES)), dma((4, PIECES)),
            dma((n,)), dma((n,)), dma((m,)), dma((m,)),
        ],
        compiler_params=pltpu.CompilerParams(
            collective_id=0, has_side_effects=True, vmem_limit_bytes=ROOM
        ),
        cost_estimate=pl.CostEstimate(
            flops=16 * slots * rows * rows * width, bytes_accessed=20 * rows * width, transcendentals=0
        ),
    )(lengths, gain.reshape(1, width), queries, keys, values, gates, grad_out)
    output, grad_q, grad_k, grad_v, grad_gate, grad_gain = pl.pallas_call(
        finish,
        out_shape=shapes,
        in_specs=[any_spec] * 6,
        out_specs=[any_spec] * 6,
        scratch_shapes=[pltpu.VMEM(x.shape, x.dtype) for x in shapes] + [dma((2, 6))],
        compiler_params=pltpu.CompilerParams(has_side_effects=True, vmem_limit_bytes=ROOM),
    )(*outs)
    return output, grad_q, grad_k, grad_v, grad_gate, grad_gain.reshape(width)


def solution(mesh):
    blocked = P("own", "seq", None)
    sizes = (mesh.shape["seq"], mesh.shape["own"])
    return jax.shard_map(
        functools.partial(per_device, *sizes),
        mesh=mesh,
        in_specs=(blocked, blocked, blocked, blocked, P("own", None), P(), blocked),
        out_specs=(blocked, blocked, blocked, blocked, blocked, P()),
        check_vma=False,
    )
```

```python
import functools
import math

import jax
import jax.numpy as jnp
from jax import lax
from jax.experimental import pallas as pl
from jax.experimental.pallas import tpu as pltpu
from jax.sharding import PartitionSpec as P

H = 8
MESH = pl.DeviceIdType.MESH
K, V, Q, G = 0, 1, 2, 3
PIECES = 8
HALVES = 2
ROOM = 60 * 1024 * 1024


def dot_nt(a, b):
    return lax.dot_general(a, b, (((1,), (1,)), ((), ())), preferred_element_type=jnp.float32)


def dot_nn(a, b):
    return lax.dot_general(a, b, (((1,), (0,)), ((), ())), preferred_element_type=jnp.float32)


def silu_and_slope(scores):
    sig = 0.5 * jnp.tanh(0.5 * scores) + 0.5
    silu = scores * sig
    return silu, sig + silu * (1.0 - sig)


def kernel(
    n, m, reach, wide, scale,
    lens_hbm, gain_hbm, q_hbm, k_hbm, v_hbm, gate_hbm, grad_hbm,
    out_hbm, gq_hbm, gk_hbm, gv_hbm, gg_hbm, ggain_hbm,
    lens_ref, gain_ref, blocks, gate, grad,
    row_probs, row_slope, col_probs, col_slope,
    far_row_probs, far_row_slope, far_col_probs, far_col_slope,
    attended, gq_sum, gk_sum, gv_sum, results,
    part, seq_parts, total, own_parts, part_sum,
    load_sem, store_sem, send_sem, recv_sem, relay_sem, seq_send, seq_recv, own_send, own_recv,
):
    me = lax.axis_index("seq")
    mine = lax.axis_index("own")
    rows, width = gate.shape
    head = width // H
    users = lens_ref.shape[1]
    groups = reach // wide
    relayed = n == 4 and reach == 2
    piece = rows // PIECES
    everything = range(PIECES)

    def near(what, h):
        return blocks[what, 0, :, h]

    def far(what, first, h):
        return blocks[what, pl.ds(first, wide), :, h].reshape(wide * rows, head)

    def far_half(what, first, wide, half, h):
        length = rows // HALVES
        return blocks[what, pl.ds(first, wide), pl.ds(half * length, length), h].reshape(wide * length, head)

    def each_head(count, body):
        @pl.loop(0, H // count)
        def _(i):
            for j in range(count):
                h = i * count + j
                body(h, pl.ds(pl.multiple_of(h * head, head), head))

    def load(i, src, dst):
        return pltpu.make_async_copy(src, dst, load_sem.at[i])

    loads = [
        load(0, k_hbm.at[0], blocks.at[K, 0]),
        load(1, v_hbm.at[0], blocks.at[V, 0]),
        load(2, q_hbm.at[0], blocks.at[Q, 0]),
        load(3, gate_hbm.at[0], gate),
        load(4, grad_hbm.at[0], grad),
        load(5, gain_hbm, gain_ref),
        load(6, lens_hbm, lens_ref),
    ]
    for copy in loads:
        copy.start()

    barrier = pltpu.get_barrier_semaphore()

    @pl.loop(1, n)
    def _(j):
        pl.semaphore_signal(barrier, 1, device_id={"seq": lax.rem(me + j, n)}, device_id_type=MESH)

    @pl.loop(1, m)
    def _(j):
        pl.semaphore_signal(barrier, 1, device_id={"own": lax.rem(mine + j, m)}, device_id_type=MESH)

    for copy in loads[:3]:
        copy.wait()
    pl.semaphore_wait(barrier, n + m - 2)

    def later(what):
        return what in (K, V)

    def span(c):
        return pl.ds(c * piece if isinstance(c, int) else pl.multiple_of(c * piece, piece), piece)

    def send(what, d, c):
        return pltpu.make_async_remote_copy(
            src_ref=blocks.at[what, 0, span(c)], dst_ref=blocks.at[what, d, span(c)],
            send_sem=send_sem.at[what, d, c], recv_sem=recv_sem.at[what, d, c],
            device_id={"seq": me + d if later(what) else me - d}, device_id_type=MESH,
        )

    def relay(what, c):
        return pltpu.make_async_remote_copy(
            src_ref=blocks.at[what, 2, span(c)], dst_ref=blocks.at[what, 1, span(c)],
            send_sem=relay_sem.at[what, c], recv_sem=recv_sem.at[what, 1, c],
            device_id={"seq": 2 if later(what) else 1}, device_id_type=MESH,
        )

    def can_send(what, d):
        ok = me + d < n if later(what) else me >= d
        if relayed and d == 1:
            ok = ok & (me != (1 if later(what) else 2))
        return ok

    def start(what, pieces):
        for d in range(1, reach + 1):
            @pl.when(can_send(what, d))
            def _():
                for c in pieces:
                    send(what, d, c).start()

    def wait_sends(what):
        for d in range(1, reach + 1):
            @pl.when(can_send(what, d))
            def _():
                for c in everything:
                    send(what, d, c).wait_send()

    def arrive(what, d, pieces=everything):
        for c in pieces:
            send(what, d, c).wait_recv()

    def arrive_and_relay(what, pieces=everything):
        for c in pieces:
            send(what, 2, c).wait_recv()
            relay(what, c).start()

    def arrive_group(what, first, pieces=everything):
        for d in range(first, first + wide):
            pl.when(me >= d if later(what) else me + d < n)(functools.partial(arrive, what, d, pieces))

    def arrive_all(what, pieces=everything):
        if relayed:
            relayer = 3 if later(what) else 0

            @pl.when(me == relayer)
            def _():
                arrive_and_relay(what, pieces)
                arrive(what, 1, pieces)

            pl.when(me != relayer)(functools.partial(arrive_group, what, 1, pieces))

    start(K, everything)
    start(V, everything)
    if relayed:
        pl.when(me != 3)(functools.partial(start, Q, everything))
    else:
        start(Q, everything)
    if relayed:
        @pl.when(me == 3)
        def _():
            for c in everything:
                send(Q, 2, c).start()
            for c in everything[: PIECES // 2]:
                send(Q, 1, c).start()

    if wide == 2:
        for d in range(2, reach + 1, 2):
            @pl.when(me == d - 1)
            def _():
                blocks[K, d] = jnp.zeros((rows, width), jnp.bfloat16)
                blocks[V, d] = jnp.zeros((rows, width), jnp.bfloat16)

    def weight(t, s):
        first = jnp.zeros_like(t)
        length = jnp.ones_like(t)
        end = jnp.int32(0)
        for u in range(users):
            begin, end = end, end + lens_ref[0, u]
            inside = (t >= begin) & (t < end)
            first = jnp.where(inside, begin, first)
            length = jnp.where(inside, lens_ref[0, u], length)
        return jnp.where((s >= first) & (s <= t), 1.0 / length.astype(jnp.float32), 0.0)

    def iotas(columns):
        return [lax.broadcasted_iota(jnp.int32, (rows, columns), i) for i in (0, 1)]

    for copy in loads[5:]:
        copy.wait()

    def pointwise(scores, w, probs_ref, slope_ref):
        scores = scores * scale
        silu, slope = silu_and_slope(scores)
        probs = (silu * w).astype(jnp.bfloat16)
        probs_ref[...] = probs
        slope_ref[...] = slope * w
        return probs

    down, across = iotas(rows)
    w = weight(me * rows + down, me * rows + across)

    def near_forward(h, at):
        probs = pointwise(dot_nt(near(Q, at), near(K, at)), w, row_probs.at[h], row_slope.at[h])
        attended[:, at] = dot_nn(probs, near(V, at))

    each_head(4, near_forward)

    near_w = weight(me * rows + across, me * rows + down)

    def near_column(h, at):
        pointwise(dot_nt(near(K, at), near(Q, at)), near_w, col_probs.at[h], col_slope.at[h])

    each_head(4, near_column)

    arrive_all(K)
    for g in range(groups):
        first = 1 + g * wide

        @pl.when(me >= first)
        def _():
            if not relayed:
                arrive_group(K, first)
            down, across = iotas(wide * rows)
            s = (me - first) * rows + across - jnp.where(across >= rows, 2 * rows, 0)
            w = weight(me * rows + down, s)

            def body(h, at):
                scores = dot_nt(near(Q, at), far(K, first, at))
                pointwise(scores, w, far_row_probs.at[g, h], far_row_slope.at[g, h])

            each_head(4, body)

    arrive_all(V)
    if relayed:
        @pl.when(me == 3)
        def _():
            for c in everything[PIECES // 2 :]:
                send(Q, 1, c).start()
    if not relayed:
        for g in range(groups):
            arrive_group(V, 1 + g * wide)

    for copy in loads[3:5]:
        copy.wait()
    gain = gain_ref[...]
    step = 32 if rows % 32 == 0 else rows

    @pl.loop(0, HALVES)
    def _(half):
        length = rows // HALVES
        part_rows = pl.ds(pl.multiple_of(half * length, length), length)
        for g in range(groups):
            first = 1 + g * wide

            @pl.when(me >= first)
            def _():
                def body(h, at):
                    attended[part_rows, at] += dot_nn(far_row_probs[g, h, part_rows, :], far(V, first, at))

                each_head(H, body)

        pieces = [half * (PIECES // HALVES) + c for c in range(PIECES // HALVES)]
        for c in pieces:
            at = span(c)
            att = attended[at, :]
            center = att - jnp.mean(att, axis=1, keepdims=True)
            rstd = lax.rsqrt(jnp.mean(center * center, axis=1, keepdims=True) + 1e-05)
            normed = center * rstd
            dnorm = grad[at, :].astype(jnp.float32) * gate[at, :].astype(jnp.float32) * gain
            back = rstd * (
                dnorm
                - jnp.mean(dnorm, axis=1, keepdims=True)
                - normed * jnp.mean(dnorm * normed, axis=1, keepdims=True)
            )
            attended[at, :] = normed
            blocks[G, 0, at, :] = back.astype(jnp.bfloat16)
        start(G, pieces)

    part[...] = jnp.zeros((1, width), jnp.float32)

    @pl.loop(0, rows // step)
    def _(i):
        at = pl.ds(pl.multiple_of(i * step, step), step)
        normed = attended[at, :]
        gate_f = gate[at, :].astype(jnp.float32)
        grad_f = grad[at, :].astype(jnp.float32)
        results[0, at, :] = (normed * gain * gate_f).astype(jnp.bfloat16)
        results[1, at, :] = (grad_f * normed * gain).astype(jnp.bfloat16)
        part[...] += jnp.sum(grad_f * gate_f * normed, axis=0, keepdims=True)

    def seq_share(j):
        return pltpu.make_async_remote_copy(
            src_ref=part, dst_ref=seq_parts.at[me],
            send_sem=seq_send.at[j], recv_sem=seq_recv.at[me],
            device_id={"seq": lax.rem(me + j, n)}, device_id_type=MESH,
        )

    def own_share(j):
        return pltpu.make_async_remote_copy(
            src_ref=total, dst_ref=own_parts.at[mine],
            send_sem=own_send.at[j], recv_sem=own_recv.at[mine],
            device_id={"own": lax.rem(mine + j, m)}, device_id_type=MESH,
        )

    pl.loop(1, n)(lambda j: seq_share(j).start())
    seq_parts[me] = part[...]

    def store(i, dst):
        return pltpu.make_async_copy(results.at[i], dst.at[0], store_sem.at[i])

    stores = [store(i, dst) for i, dst in enumerate((out_hbm, gg_hbm, gq_hbm, gk_hbm, gv_hbm))]
    stores[0].start()
    stores[1].start()

    def near_back(h, at):
        grad_probs = dot_nt(near(G, at), near(V, at))
        gq_sum[:, at] = dot_nn((grad_probs * row_slope[h]).astype(jnp.bfloat16), near(K, at))
        grad_probs = dot_nt(near(V, at), near(G, at))
        gk_sum[:, at] = dot_nn((grad_probs * col_slope[h]).astype(jnp.bfloat16), near(Q, at))
        gv_sum[:, at] = dot_nn(col_probs[h], near(G, at))

    each_head(4, near_back)
    for g in range(groups):
        first = 1 + g * wide

        @pl.when(me >= first)
        def _():
            def body(h, at):
                grad_probs = dot_nt(near(G, at), far(V, first, at))
                grad_scores = (grad_probs * far_row_slope[g, h]).astype(jnp.bfloat16)
                gq_sum[:, at] += dot_nn(grad_scores, far(K, first, at))

            each_head(4, body)

    results[2] = (gq_sum[...] * scale).astype(jnp.bfloat16)
    stores[2].start()

    def columns(first, body):
        if wide == 2:
            pl.when(me + first + 1 < n)(functools.partial(body, 2))
            pl.when(me + first + 1 == n)(functools.partial(body, 1))
        else:
            pl.when(me + first < n)(functools.partial(body, 1))

    def far_column(g, first, slots):
        count = slots * rows // HALVES
        down, across = iotas(count)
        lanes = pl.ds(0, count)
        for half in range(HALVES):
            t = (me + first) * rows + half * (rows // HALVES) + across
            if slots == 2:
                t = t + jnp.where(across >= rows // HALVES, rows - rows // HALVES, 0)
            w = weight(t, me * rows + down)

            def body(h, at):
                scores = dot_nt(near(K, at), far_half(Q, first, slots, half, at))
                pointwise(scores, w, far_col_probs.at[g, half, h, :, lanes], far_col_slope.at[g, half, h, :, lanes])

            each_head(4, body)

    def far_column_back(g, first, half, slots):
        lanes = pl.ds(0, slots * rows // HALVES)

        def body(h, at):
            back = far_half(G, first, slots, half, at)
            grad_probs = dot_nt(near(V, at), back)
            grad_scores = (grad_probs * far_col_slope[g, half, h, :, lanes]).astype(jnp.bfloat16)
            key_sum = gk_sum[:, at] + dot_nn(grad_scores, far_half(Q, first, slots, half, at))
            value_sum = gv_sum[:, at] + dot_nn(far_col_probs[g, half, h, :, lanes], back)
            if groups == 1 and half == HALVES - 1:
                results[3, :, at] = (key_sum * scale).astype(jnp.bfloat16)
                results[4, :, at] = value_sum.astype(jnp.bfloat16)
            else:
                gk_sum[:, at] = key_sum
                gv_sum[:, at] = value_sum

        each_head(4, body)

    def sum_over_seq():
        @pl.loop(1, n)
        def _(j):
            src = lax.rem(me + j, n)
            pltpu.make_async_remote_copy(
                src_ref=part, dst_ref=seq_parts.at[src],
                send_sem=seq_send.at[j], recv_sem=seq_recv.at[src],
                device_id={"seq": src}, device_id_type=MESH,
            ).wait_recv()

        group = seq_parts[0]
        for j in range(1, n):
            group = group + seq_parts[j]
        total[...] = group
        pl.loop(1, m)(lambda j: own_share(j).start())
        own_parts[mine] = group

    wait_sends(V)
    arrive_all(Q)
    for g in range(groups):
        first = 1 + g * wide
        if not relayed:
            arrive_group(Q, first)
        columns(first, functools.partial(far_column, g, first))

    for half in range(HALVES):
        pieces = everything[half * PIECES // HALVES : (half + 1) * PIECES // HALVES]
        arrive_all(G, pieces)
        if half == 0:
            sum_over_seq()
        for g in range(groups):
            first = 1 + g * wide
            if not relayed:
                arrive_group(G, first, pieces)
            columns(first, functools.partial(far_column_back, g, first, half))

    @pl.when((me == n - 1) | (groups > 1))
    def _():
        results[3] = (gk_sum[...] * scale).astype(jnp.bfloat16)
        results[4] = gv_sum[...].astype(jnp.bfloat16)

    stores[3].start()
    stores[4].start()

    @pl.loop(1, m)
    def _(j):
        src = lax.rem(mine + j, m)
        pltpu.make_async_remote_copy(
            src_ref=total, dst_ref=own_parts.at[src],
            send_sem=own_send.at[j], recv_sem=own_recv.at[src],
            device_id={"own": src}, device_id_type=MESH,
        ).wait_recv()

    whole = own_parts[0]
    for j in range(1, m):
        whole = whole + own_parts[j]
    part_sum[...] = whole
    last = pltpu.make_async_copy(part_sum, ggain_hbm, store_sem.at[5])
    last.start()

    for what in (K, V, Q, G):
        if what != V:
            wait_sends(what)
        if relayed:
            @pl.when(me == (3 if later(what) else 0))
            def _():
                for c in everything:
                    relay(what, c).wait_send()
    pl.loop(1, n)(lambda j: seq_share(j).wait_send())
    pl.loop(1, m)(lambda j: own_share(j).wait_send())
    for copy in stores + [last]:
        copy.wait()


def finish(*refs):
    sources, results, held, sem = refs[:6], refs[6:12], refs[12:18], refs[18]
    loads = [pltpu.make_async_copy(a, b, sem.at[0, i]) for i, (a, b) in enumerate(zip(sources, held))]
    stores = [pltpu.make_async_copy(a, b, sem.at[1, i]) for i, (a, b) in enumerate(zip(held, results))]
    for copy in loads:
        copy.start()
    for load, store in zip(loads, stores):
        load.wait()
        store.start()
    for copy in stores:
        copy.wait()


def per_device(n, m, queries, keys, values, gates, lengths, gain, grad_out):
    rows, width = queries.shape[1], queries.shape[2]
    head = width // H
    reach = min(n - 1, (rows * n // 2 - 1) // rows + 1)
    slots = reach + 1
    wide = 2 if reach % 2 == 0 else 1
    groups = reach // wide
    hbm = pl.BlockSpec(memory_space=pltpu.HBM)
    any_spec = pl.BlockSpec(memory_space=pl.ANY)
    block = jax.ShapeDtypeStruct(queries.shape, jnp.bfloat16)
    shapes = [block] * 5 + [jax.ShapeDtypeStruct((1, width), jnp.float32)]
    dma = pltpu.SemaphoreType.DMA
    outs = pl.pallas_call(
        functools.partial(kernel, n, m, reach, wide, 1.0 / math.sqrt(head)),
        out_shape=shapes,
        in_specs=[hbm] * 7,
        out_specs=[any_spec] * 6,
        scratch_shapes=[
            pltpu.SMEM(lengths.shape, jnp.int32),
            pltpu.VMEM((1, width), jnp.float32),
            pltpu.VMEM((4, slots, rows, width), jnp.bfloat16),
            pltpu.VMEM((rows, width), jnp.bfloat16),
            pltpu.VMEM((rows, width), jnp.bfloat16),
            pltpu.VMEM((H, rows, rows), jnp.bfloat16),
            pltpu.VMEM((H, rows, rows), jnp.float32),
            pltpu.VMEM((H, rows, rows), jnp.bfloat16),
            pltpu.VMEM((H, rows, rows), jnp.float32),
            pltpu.VMEM((groups, H, rows, wide * rows), jnp.bfloat16),
            pltpu.VMEM((groups, H, rows, wide * rows), jnp.float32),
            pltpu.VMEM((groups, HALVES, H, rows, wide * rows // HALVES), jnp.bfloat16),
            pltpu.VMEM((groups, HALVES, H, rows, wide * rows // HALVES), jnp.float32),
            pltpu.VMEM((rows, width), jnp.float32),
            pltpu.VMEM((rows, width), jnp.float32),
            pltpu.VMEM((rows, width), jnp.float32),
            pltpu.VMEM((rows, width), jnp.float32),
            pltpu.VMEM((5, rows, width), jnp.bfloat16),
            pltpu.VMEM((1, width), jnp.float32),
            pltpu.VMEM((n, 1, width), jnp.float32),
            pltpu.VMEM((1, width), jnp.float32),
            pltpu.VMEM((m, 1, width), jnp.float32),
            pltpu.VMEM((1, width), jnp.float32),
            dma((7,)), dma((6,)), dma((4, slots, PIECES)), dma((4, slots, PIECES)), dma((4, PIECES)),
            dma((n,)), dma((n,)), dma((m,)), dma((m,)),
        ],
        compiler_params=pltpu.CompilerParams(
            collective_id=0, has_side_effects=True, vmem_limit_bytes=ROOM
        ),
        cost_estimate=pl.CostEstimate(
            flops=16 * slots * rows * rows * width, bytes_accessed=20 * rows * width, transcendentals=0
        ),
    )(lengths, gain.reshape(1, width), queries, keys, values, gates, grad_out)
    output, grad_q, grad_k, grad_v, grad_gate, grad_gain = pl.pallas_call(
        finish,
        out_shape=shapes,
        in_specs=[any_spec] * 6,
        out_specs=[any_spec] * 6,
        scratch_shapes=[pltpu.VMEM(x.shape, x.dtype) for x in shapes] + [dma((2, 6))],
        compiler_params=pltpu.CompilerParams(has_side_effects=True, vmem_limit_bytes=ROOM),
    )(*outs)
    return output, grad_q, grad_k, grad_v, grad_gate, grad_gain.reshape(width)


def solution(mesh):
    blocked = P("own", "seq", None)
    sizes = (mesh.shape["seq"], mesh.shape["own"])
    return jax.shard_map(
        functools.partial(per_device, *sizes),
        mesh=mesh,
        in_specs=(blocked, blocked, blocked, blocked, P("own", None), P(), blocked),
        out_specs=(blocked, blocked, blocked, blocked, blocked, P()),
        check_vma=False,
    )
```

```python
import functools
import math

import jax
import jax.numpy as jnp
from jax import lax
from jax.experimental import pallas as pl
from jax.experimental.pallas import tpu as pltpu
from jax.sharding import PartitionSpec as P

H = 8
MESH = pl.DeviceIdType.MESH
K, V, Q, G = 0, 1, 2, 3
PIECES = 2
HALVES = 2
ROOM = 60 * 1024 * 1024


def dot_nt(a, b):
    return lax.dot_general(a, b, (((1,), (1,)), ((), ())), preferred_element_type=jnp.float32)


def dot_nn(a, b):
    return lax.dot_general(a, b, (((1,), (0,)), ((), ())), preferred_element_type=jnp.float32)


def silu_and_slope(scores):
    sig = 0.5 * jnp.tanh(0.5 * scores) + 0.5
    silu = scores * sig
    return silu, sig + silu * (1.0 - sig)


def kernel(
    n, m, reach, wide, scale,
    lens_hbm, gain_hbm, q_hbm, k_hbm, v_hbm, gate_hbm, grad_hbm,
    out_hbm, gq_hbm, gk_hbm, gv_hbm, gg_hbm, ggain_hbm,
    lens_ref, gain_ref, blocks, gate, grad,
    row_probs, row_slope, col_probs, col_slope,
    far_row_probs, far_row_slope, far_col_probs, far_col_slope,
    attended, gq_sum, gk_sum, gv_sum, results,
    part, seq_parts, total, own_parts, part_sum,
    load_sem, store_sem, send_sem, recv_sem, relay_sem, seq_send, seq_recv, own_send, own_recv,
):
    me = lax.axis_index("seq")
    mine = lax.axis_index("own")
    rows, width = gate.shape
    head = width // H
    users = lens_ref.shape[1]
    groups = reach // wide
    relayed = n == 4 and reach == 2
    piece = rows // PIECES
    everything = range(PIECES)

    def near(what, h):
        return blocks[what, 0, :, h]

    def far(what, first, h):
        return blocks[what, pl.ds(first, wide), :, h].reshape(wide * rows, head)

    def far_half(what, first, wide, half, h):
        length = rows // HALVES
        return blocks[what, pl.ds(first, wide), pl.ds(half * length, length), h].reshape(wide * length, head)

    def each_head(count, body):
        @pl.loop(0, H // count)
        def _(i):
            for j in range(count):
                h = i * count + j
                body(h, pl.ds(pl.multiple_of(h * head, head), head))

    def load(i, src, dst):
        return pltpu.make_async_copy(src, dst, load_sem.at[i])

    loads = [
        load(0, k_hbm.at[0], blocks.at[K, 0]),
        load(1, v_hbm.at[0], blocks.at[V, 0]),
        load(2, q_hbm.at[0], blocks.at[Q, 0]),
        load(3, gate_hbm.at[0], gate),
        load(4, grad_hbm.at[0], grad),
        load(5, gain_hbm, gain_ref),
        load(6, lens_hbm, lens_ref),
    ]
    for copy in loads:
        copy.start()

    barrier = pltpu.get_barrier_semaphore()

    @pl.loop(1, n)
    def _(j):
        pl.semaphore_signal(barrier, 1, device_id={"seq": lax.rem(me + j, n)}, device_id_type=MESH)

    @pl.loop(1, m)
    def _(j):
        pl.semaphore_signal(barrier, 1, device_id={"own": lax.rem(mine + j, m)}, device_id_type=MESH)

    for copy in loads[:3]:
        copy.wait()
    pl.semaphore_wait(barrier, n + m - 2)

    def later(what):
        return what in (K, V)

    def span(c):
        return pl.ds(c * piece if isinstance(c, int) else pl.multiple_of(c * piece, piece), piece)

    def send(what, d, c):
        return pltpu.make_async_remote_copy(
            src_ref=blocks.at[what, 0, span(c)], dst_ref=blocks.at[what, d, span(c)],
            send_sem=send_sem.at[what, d, c], recv_sem=recv_sem.at[what, d, c],
            device_id={"seq": me + d if later(what) else me - d}, device_id_type=MESH,
        )

    def relay(what, c):
        return pltpu.make_async_remote_copy(
            src_ref=blocks.at[what, 2, span(c)], dst_ref=blocks.at[what, 1, span(c)],
            send_sem=relay_sem.at[what, c], recv_sem=recv_sem.at[what, 1, c],
            device_id={"seq": 2 if later(what) else 1}, device_id_type=MESH,
        )

    def can_send(what, d):
        ok = me + d < n if later(what) else me >= d
        if relayed and d == 1:
            ok = ok & (me != (1 if later(what) else 2))
        return ok

    def start(what, pieces):
        for d in range(1, reach + 1):
            @pl.when(can_send(what, d))
            def _():
                for c in pieces:
                    send(what, d, c).start()

    def wait_sends(what):
        for d in range(1, reach + 1):
            @pl.when(can_send(what, d))
            def _():
                for c in everything:
                    send(what, d, c).wait_send()

    def arrive(what, d, pieces=everything):
        for c in pieces:
            send(what, d, c).wait_recv()

    def arrive_and_relay(what, pieces=everything):
        for c in pieces:
            send(what, 2, c).wait_recv()
            relay(what, c).start()

    def arrive_group(what, first, pieces=everything):
        for d in range(first, first + wide):
            pl.when(me >= d if later(what) else me + d < n)(functools.partial(arrive, what, d, pieces))

    def arrive_all(what, pieces=everything):
        if relayed:
            relayer = 3 if later(what) else 0

            @pl.when(me == relayer)
            def _():
                arrive_and_relay(what, pieces)
                arrive(what, 1, pieces)

            pl.when(me != relayer)(functools.partial(arrive_group, what, 1, pieces))

    start(K, everything)
    start(V, everything)
    if relayed:
        pl.when(me != 3)(functools.partial(start, Q, everything))
    else:
        start(Q, everything)
    if relayed:
        @pl.when(me == 3)
        def _():
            for c in everything:
                send(Q, 2, c).start()
            for c in everything[: PIECES // 2]:
                send(Q, 1, c).start()

    if wide == 2:
        for d in range(2, reach + 1, 2):
            @pl.when(me == d - 1)
            def _():
                blocks[K, d] = jnp.zeros((rows, width), jnp.bfloat16)
                blocks[V, d] = jnp.zeros((rows, width), jnp.bfloat16)

    def weight(t, s):
        first = jnp.zeros_like(t)
        length = jnp.ones_like(t)
        end = jnp.int32(0)
        for u in range(users):
            begin, end = end, end + lens_ref[0, u]
            inside = (t >= begin) & (t < end)
            first = jnp.where(inside, begin, first)
            length = jnp.where(inside, lens_ref[0, u], length)
        return jnp.where((s >= first) & (s <= t), 1.0 / length.astype(jnp.float32), 0.0)

    def iotas(columns):
        return [lax.broadcasted_iota(jnp.int32, (rows, columns), i) for i in (0, 1)]

    for copy in loads[5:]:
        copy.wait()

    def pointwise(scores, w, probs_ref, slope_ref):
        scores = scores * scale
        silu, slope = silu_and_slope(scores)
        probs = (silu * w).astype(jnp.bfloat16)
        probs_ref[...] = probs
        slope_ref[...] = slope * w
        return probs

    down, across = iotas(rows)
    w = weight(me * rows + down, me * rows + across)

    def near_forward(h, at):
        probs = pointwise(dot_nt(near(Q, at), near(K, at)), w, row_probs.at[h], row_slope.at[h])
        attended[:, at] = dot_nn(probs, near(V, at))

    each_head(4, near_forward)

    near_w = weight(me * rows + across, me * rows + down)

    def near_column(h, at):
        pointwise(dot_nt(near(K, at), near(Q, at)), near_w, col_probs.at[h], col_slope.at[h])

    each_head(4, near_column)

    arrive_all(K)
    for g in range(groups):
        first = 1 + g * wide

        @pl.when(me >= first)
        def _():
            if not relayed:
                arrive_group(K, first)
            down, across = iotas(wide * rows)
            s = (me - first) * rows + across - jnp.where(across >= rows, 2 * rows, 0)
            w = weight(me * rows + down, s)

            def body(h, at):
                scores = dot_nt(near(Q, at), far(K, first, at))
                pointwise(scores, w, far_row_probs.at[g, h], far_row_slope.at[g, h])

            each_head(4, body)

    arrive_all(V)
    if relayed:
        @pl.when(me == 3)
        def _():
            for c in everything[PIECES // 2 :]:
                send(Q, 1, c).start()
    if not relayed:
        for g in range(groups):
            arrive_group(V, 1 + g * wide)

    for copy in loads[3:5]:
        copy.wait()
    gain = gain_ref[...]
    step = math.gcd(32, rows // HALVES)

    @pl.loop(0, HALVES)
    def _(half):
        length = rows // HALVES
        part_rows = pl.ds(pl.multiple_of(half * length, length), length)
        for g in range(groups):
            first = 1 + g * wide

            @pl.when(me >= first)
            def _():
                def body(h, at):
                    attended[part_rows, at] += dot_nn(far_row_probs[g, h, part_rows, :], far(V, first, at))

                each_head(H, body)

        pieces = [half * (PIECES // HALVES) + c for c in range(PIECES // HALVES)]
        for r in range(0, length, step):
            at = pl.ds(pl.multiple_of(half * length + r, step), step)
            att = attended[at, :]
            center = att - jnp.mean(att, axis=1, keepdims=True)
            rstd = lax.rsqrt(jnp.mean(center * center, axis=1, keepdims=True) + 1e-05)
            normed = center * rstd
            dnorm = grad[at, :].astype(jnp.float32) * gate[at, :].astype(jnp.float32) * gain
            back = rstd * (
                dnorm
                - jnp.mean(dnorm, axis=1, keepdims=True)
                - normed * jnp.mean(dnorm * normed, axis=1, keepdims=True)
            )
            attended[at, :] = normed
            blocks[G, 0, at, :] = back.astype(jnp.bfloat16)
        start(G, pieces)

    part[...] = jnp.zeros((1, width), jnp.float32)

    @pl.loop(0, rows // step)
    def _(i):
        at = pl.ds(pl.multiple_of(i * step, step), step)
        normed = attended[at, :]
        gate_f = gate[at, :].astype(jnp.float32)
        grad_f = grad[at, :].astype(jnp.float32)
        results[0, at, :] = (normed * gain * gate_f).astype(jnp.bfloat16)
        results[1, at, :] = (grad_f * normed * gain).astype(jnp.bfloat16)
        part[...] += jnp.sum(grad_f * gate_f * normed, axis=0, keepdims=True)

    def seq_share(j):
        return pltpu.make_async_remote_copy(
            src_ref=part, dst_ref=seq_parts.at[me],
            send_sem=seq_send.at[j], recv_sem=seq_recv.at[me],
            device_id={"seq": lax.rem(me + j, n)}, device_id_type=MESH,
        )

    def own_share(j):
        return pltpu.make_async_remote_copy(
            src_ref=total, dst_ref=own_parts.at[mine],
            send_sem=own_send.at[j], recv_sem=own_recv.at[mine],
            device_id={"own": lax.rem(mine + j, m)}, device_id_type=MESH,
        )

    pl.loop(1, n)(lambda j: seq_share(j).start())
    seq_parts[me] = part[...]

    def store(i, dst):
        return pltpu.make_async_copy(results.at[i], dst.at[0], store_sem.at[i])

    stores = [store(i, dst) for i, dst in enumerate((out_hbm, gg_hbm, gq_hbm, gk_hbm, gv_hbm))]
    stores[0].start()
    stores[1].start()

    def near_back(h, at):
        grad_probs = dot_nt(near(G, at), near(V, at))
        gq_sum[:, at] = dot_nn((grad_probs * row_slope[h]).astype(jnp.bfloat16), near(K, at))
        grad_probs = dot_nt(near(V, at), near(G, at))
        gk_sum[:, at] = dot_nn((grad_probs * col_slope[h]).astype(jnp.bfloat16), near(Q, at))
        gv_sum[:, at] = dot_nn(col_probs[h], near(G, at))

    each_head(4, near_back)
    for g in range(groups):
        first = 1 + g * wide

        @pl.when(me >= first)
        def _():
            def body(h, at):
                grad_probs = dot_nt(near(G, at), far(V, first, at))
                grad_scores = (grad_probs * far_row_slope[g, h]).astype(jnp.bfloat16)
                gq_sum[:, at] += dot_nn(grad_scores, far(K, first, at))

            each_head(4, body)

    results[2] = (gq_sum[...] * scale).astype(jnp.bfloat16)
    stores[2].start()

    def columns(first, body):
        if wide == 2:
            pl.when(me + first + 1 < n)(functools.partial(body, 2))
            pl.when(me + first + 1 == n)(functools.partial(body, 1))
        else:
            pl.when(me + first < n)(functools.partial(body, 1))

    def far_column(g, first, slots):
        count = slots * rows // HALVES
        down, across = iotas(count)
        lanes = pl.ds(0, count)
        for half in range(HALVES):
            t = (me + first) * rows + half * (rows // HALVES) + across
            if slots == 2:
                t = t + jnp.where(across >= rows // HALVES, rows - rows // HALVES, 0)
            w = weight(t, me * rows + down)

            def body(h, at):
                scores = dot_nt(near(K, at), far_half(Q, first, slots, half, at))
                pointwise(scores, w, far_col_probs.at[g, half, h, :, lanes], far_col_slope.at[g, half, h, :, lanes])

            each_head(4, body)

    def far_column_back(g, first, half, slots):
        lanes = pl.ds(0, slots * rows // HALVES)

        def body(h, at):
            back = far_half(G, first, slots, half, at)
            grad_probs = dot_nt(near(V, at), back)
            grad_scores = (grad_probs * far_col_slope[g, half, h, :, lanes]).astype(jnp.bfloat16)
            key_sum = gk_sum[:, at] + dot_nn(grad_scores, far_half(Q, first, slots, half, at))
            value_sum = gv_sum[:, at] + dot_nn(far_col_probs[g, half, h, :, lanes], back)
            if groups == 1 and half == HALVES - 1:
                results[3, :, at] = (key_sum * scale).astype(jnp.bfloat16)
                results[4, :, at] = value_sum.astype(jnp.bfloat16)
            else:
                gk_sum[:, at] = key_sum
                gv_sum[:, at] = value_sum

        each_head(4, body)

    def sum_over_seq():
        @pl.loop(1, n)
        def _(j):
            src = lax.rem(me + j, n)
            pltpu.make_async_remote_copy(
                src_ref=part, dst_ref=seq_parts.at[src],
                send_sem=seq_send.at[j], recv_sem=seq_recv.at[src],
                device_id={"seq": src}, device_id_type=MESH,
            ).wait_recv()

        group = seq_parts[0]
        for j in range(1, n):
            group = group + seq_parts[j]
        total[...] = group
        pl.loop(1, m)(lambda j: own_share(j).start())
        own_parts[mine] = group

    wait_sends(V)
    arrive_all(Q)
    for g in range(groups):
        first = 1 + g * wide
        if not relayed:
            arrive_group(Q, first)
        columns(first, functools.partial(far_column, g, first))

    for half in range(HALVES):
        pieces = everything[half * PIECES // HALVES : (half + 1) * PIECES // HALVES]
        arrive_all(G, pieces)
        if half == 0:
            sum_over_seq()
        for g in range(groups):
            first = 1 + g * wide
            if not relayed:
                arrive_group(G, first, pieces)
            columns(first, functools.partial(far_column_back, g, first, half))

    @pl.when((me == n - 1) | (groups > 1))
    def _():
        results[3] = (gk_sum[...] * scale).astype(jnp.bfloat16)
        results[4] = gv_sum[...].astype(jnp.bfloat16)

    stores[3].start()
    stores[4].start()

    @pl.loop(1, m)
    def _(j):
        src = lax.rem(mine + j, m)
        pltpu.make_async_remote_copy(
            src_ref=total, dst_ref=own_parts.at[src],
            send_sem=own_send.at[j], recv_sem=own_recv.at[src],
            device_id={"own": src}, device_id_type=MESH,
        ).wait_recv()

    whole = own_parts[0]
    for j in range(1, m):
        whole = whole + own_parts[j]
    part_sum[...] = whole
    last = pltpu.make_async_copy(part_sum, ggain_hbm, store_sem.at[5])
    last.start()

    for what in (K, V, Q, G):
        if what != V:
            wait_sends(what)
        if relayed:
            @pl.when(me == (3 if later(what) else 0))
            def _():
                for c in everything:
                    relay(what, c).wait_send()
    pl.loop(1, n)(lambda j: seq_share(j).wait_send())
    pl.loop(1, m)(lambda j: own_share(j).wait_send())
    for copy in stores + [last]:
        copy.wait()


def finish(*refs):
    sources, results, held, sem = refs[:6], refs[6:12], refs[12:18], refs[18]
    loads = [pltpu.make_async_copy(a, b, sem.at[0, i]) for i, (a, b) in enumerate(zip(sources, held))]
    stores = [pltpu.make_async_copy(a, b, sem.at[1, i]) for i, (a, b) in enumerate(zip(held, results))]
    for copy in loads:
        copy.start()
    for load, store in zip(loads, stores):
        load.wait()
        store.start()
    for copy in stores:
        copy.wait()


def per_device(n, m, queries, keys, values, gates, lengths, gain, grad_out):
    rows, width = queries.shape[1], queries.shape[2]
    head = width // H
    reach = min(n - 1, (rows * n // 2 - 1) // rows + 1)
    slots = reach + 1
    wide = 2 if reach % 2 == 0 else 1
    groups = reach // wide
    hbm = pl.BlockSpec(memory_space=pltpu.HBM)
    any_spec = pl.BlockSpec(memory_space=pl.ANY)
    block = jax.ShapeDtypeStruct(queries.shape, jnp.bfloat16)
    shapes = [block] * 5 + [jax.ShapeDtypeStruct((1, width), jnp.float32)]
    dma = pltpu.SemaphoreType.DMA
    outs = pl.pallas_call(
        functools.partial(kernel, n, m, reach, wide, 1.0 / math.sqrt(head)),
        out_shape=shapes,
        in_specs=[hbm] * 7,
        out_specs=[any_spec] * 6,
        scratch_shapes=[
            pltpu.SMEM(lengths.shape, jnp.int32),
            pltpu.VMEM((1, width), jnp.float32),
            pltpu.VMEM((4, slots, rows, width), jnp.bfloat16),
            pltpu.VMEM((rows, width), jnp.bfloat16),
            pltpu.VMEM((rows, width), jnp.bfloat16),
            pltpu.VMEM((H, rows, rows), jnp.bfloat16),
            pltpu.VMEM((H, rows, rows), jnp.float32),
            pltpu.VMEM((H, rows, rows), jnp.bfloat16),
            pltpu.VMEM((H, rows, rows), jnp.float32),
            pltpu.VMEM((groups, H, rows, wide * rows), jnp.bfloat16),
            pltpu.VMEM((groups, H, rows, wide * rows), jnp.float32),
            pltpu.VMEM((groups, HALVES, H, rows, wide * rows // HALVES), jnp.bfloat16),
            pltpu.VMEM((groups, HALVES, H, rows, wide * rows // HALVES), jnp.float32),
            pltpu.VMEM((rows, width), jnp.float32),
            pltpu.VMEM((rows, width), jnp.float32),
            pltpu.VMEM((rows, width), jnp.float32),
            pltpu.VMEM((rows, width), jnp.float32),
            pltpu.VMEM((5, rows, width), jnp.bfloat16),
            pltpu.VMEM((1, width), jnp.float32),
            pltpu.VMEM((n, 1, width), jnp.float32),
            pltpu.VMEM((1, width), jnp.float32),
            pltpu.VMEM((m, 1, width), jnp.float32),
            pltpu.VMEM((1, width), jnp.float32),
            dma((7,)), dma((6,)), dma((4, slots, PIECES)), dma((4, slots, PIECES)), dma((4, PIECES)),
            dma((n,)), dma((n,)), dma((m,)), dma((m,)),
        ],
        compiler_params=pltpu.CompilerParams(
            collective_id=0, has_side_effects=True, vmem_limit_bytes=ROOM
        ),
        cost_estimate=pl.CostEstimate(
            flops=16 * slots * rows * rows * width, bytes_accessed=20 * rows * width, transcendentals=0
        ),
    )(lengths, gain.reshape(1, width), queries, keys, values, gates, grad_out)
    output, grad_q, grad_k, grad_v, grad_gate, grad_gain = pl.pallas_call(
        finish,
        out_shape=shapes,
        in_specs=[any_spec] * 6,
        out_specs=[any_spec] * 6,
        scratch_shapes=[pltpu.VMEM(x.shape, x.dtype) for x in shapes] + [dma((2, 6))],
        compiler_params=pltpu.CompilerParams(has_side_effects=True, vmem_limit_bytes=ROOM),
    )(*outs)
    return output, grad_q, grad_k, grad_v, grad_gate, grad_gain.reshape(width)


def solution(mesh):
    blocked = P("own", "seq", None)
    sizes = (mesh.shape["seq"], mesh.shape["own"])
    return jax.shard_map(
        functools.partial(per_device, *sizes),
        mesh=mesh,
        in_specs=(blocked, blocked, blocked, blocked, P("own", None), P(), blocked),
        out_specs=(blocked, blocked, blocked, blocked, blocked, P()),
        check_vma=False,
    )
```

```python
import functools
import math

import jax
import jax.numpy as jnp
from jax import lax
from jax.experimental import pallas as pl
from jax.experimental.pallas import tpu as pltpu
from jax.sharding import PartitionSpec as P

H = 8
MESH = pl.DeviceIdType.MESH
K, V, Q, G = 0, 1, 2, 3
PIECES = 4
HALVES = 2
ROOM = 60 * 1024 * 1024


def dot_nt(a, b):
    return lax.dot_general(a, b, (((1,), (1,)), ((), ())), preferred_element_type=jnp.float32)


def dot_nn(a, b):
    return lax.dot_general(a, b, (((1,), (0,)), ((), ())), preferred_element_type=jnp.float32)


def silu_and_slope(scores):
    sig = 0.5 * jnp.tanh(0.5 * scores) + 0.5
    silu = scores * sig
    return silu, sig + silu * (1.0 - sig)


def kernel(
    n, m, reach, wide, scale,
    lens_hbm, gain_hbm, q_hbm, k_hbm, v_hbm, gate_hbm, grad_hbm,
    out_hbm, gq_hbm, gk_hbm, gv_hbm, gg_hbm, ggain_hbm,
    lens_ref, gain_ref, blocks, gate, grad,
    row_probs, row_slope, col_probs, col_slope,
    far_row_probs, far_row_slope, far_col_probs, far_col_slope,
    attended, gq_sum, gk_sum, gv_sum, results,
    part, seq_parts, total, own_parts, part_sum,
    load_sem, store_sem, send_sem, recv_sem, relay_sem, seq_send, seq_recv, own_send, own_recv,
):
    me = lax.axis_index("seq")
    mine = lax.axis_index("own")
    rows, width = gate.shape
    head = width // H
    users = lens_ref.shape[1]
    groups = reach // wide
    relayed = n == 4 and reach == 2
    piece = rows // PIECES
    everything = range(PIECES)

    def near(what, h):
        return blocks[what, 0, :, h]

    def far(what, first, h):
        return blocks[what, pl.ds(first, wide), :, h].reshape(wide * rows, head)

    def far_half(what, first, wide, half, h):
        length = rows // HALVES
        return blocks[what, pl.ds(first, wide), pl.ds(half * length, length), h].reshape(wide * length, head)

    def each_head(count, body):
        @pl.loop(0, H // count)
        def _(i):
            for j in range(count):
                h = i * count + j
                body(h, pl.ds(pl.multiple_of(h * head, head), head))

    def load(i, src, dst):
        return pltpu.make_async_copy(src, dst, load_sem.at[i])

    loads = [
        load(0, k_hbm.at[0], blocks.at[K, 0]),
        load(1, v_hbm.at[0], blocks.at[V, 0]),
        load(2, q_hbm.at[0], blocks.at[Q, 0]),
        load(3, gate_hbm.at[0], gate),
        load(4, grad_hbm.at[0], grad),
        load(5, gain_hbm, gain_ref),
        load(6, lens_hbm, lens_ref),
    ]
    for copy in loads:
        copy.start()

    barrier = pltpu.get_barrier_semaphore()

    @pl.loop(1, n)
    def _(j):
        pl.semaphore_signal(barrier, 1, device_id={"seq": lax.rem(me + j, n)}, device_id_type=MESH)

    @pl.loop(1, m)
    def _(j):
        pl.semaphore_signal(barrier, 1, device_id={"own": lax.rem(mine + j, m)}, device_id_type=MESH)

    for copy in loads[:3]:
        copy.wait()
    pl.semaphore_wait(barrier, n + m - 2)

    def later(what):
        return what in (K, V)

    def span(c):
        return pl.ds(c * piece if isinstance(c, int) else pl.multiple_of(c * piece, piece), piece)

    def send(what, d, c):
        return pltpu.make_async_remote_copy(
            src_ref=blocks.at[what, 0, span(c)], dst_ref=blocks.at[what, d, span(c)],
            send_sem=send_sem.at[what, d, c], recv_sem=recv_sem.at[what, d, c],
            device_id={"seq": me + d if later(what) else me - d}, device_id_type=MESH,
        )

    def relay(what, c):
        return pltpu.make_async_remote_copy(
            src_ref=blocks.at[what, 2, span(c)], dst_ref=blocks.at[what, 1, span(c)],
            send_sem=relay_sem.at[what, c], recv_sem=recv_sem.at[what, 1, c],
            device_id={"seq": 2 if later(what) else 1}, device_id_type=MESH,
        )

    def can_send(what, d):
        ok = me + d < n if later(what) else me >= d
        if relayed and d == 1:
            ok = ok & (me != (1 if later(what) else 2))
        return ok

    def start(what, pieces):
        for d in range(1, reach + 1):
            @pl.when(can_send(what, d))
            def _():
                for c in pieces:
                    send(what, d, c).start()

    def wait_sends(what):
        for d in range(1, reach + 1):
            @pl.when(can_send(what, d))
            def _():
                for c in everything:
                    send(what, d, c).wait_send()

    def arrive(what, d, pieces=everything):
        for c in pieces:
            send(what, d, c).wait_recv()

    def arrive_and_relay(what, pieces=everything):
        for c in pieces:
            send(what, 2, c).wait_recv()
            relay(what, c).start()

    def arrive_group(what, first, pieces=everything):
        for d in range(first, first + wide):
            pl.when(me >= d if later(what) else me + d < n)(functools.partial(arrive, what, d, pieces))

    def arrive_all(what, pieces=everything):
        if relayed:
            relayer = 3 if later(what) else 0

            @pl.when(me == relayer)
            def _():
                arrive_and_relay(what, pieces)
                arrive(what, 1, pieces)

            pl.when(me != relayer)(functools.partial(arrive_group, what, 1, pieces))

    start(K, everything)
    start(V, everything)
    if relayed:
        pl.when(me != 3)(functools.partial(start, Q, everything))

        @pl.when(me == 3)
        def _():
            for c in everything:
                send(Q, 2, c).start()
            for c in everything[: PIECES // 2]:
                send(Q, 1, c).start()
    else:
        start(Q, everything)

    if wide == 2:
        for d in range(2, reach + 1, 2):
            @pl.when(me == d - 1)
            def _():
                blocks[K, d] = jnp.zeros((rows, width), jnp.bfloat16)
                blocks[V, d] = jnp.zeros((rows, width), jnp.bfloat16)

    def weight(t, s):
        first = jnp.zeros_like(t)
        length = jnp.ones_like(t)
        end = jnp.int32(0)
        for u in range(users):
            begin, end = end, end + lens_ref[0, u]
            inside = (t >= begin) & (t < end)
            first = jnp.where(inside, begin, first)
            length = jnp.where(inside, lens_ref[0, u], length)
        return jnp.where((s >= first) & (s <= t), 1.0 / length.astype(jnp.float32), 0.0)

    def iotas(columns):
        return [lax.broadcasted_iota(jnp.int32, (rows, columns), i) for i in (0, 1)]

    for copy in loads[5:]:
        copy.wait()

    def pointwise(scores, w, probs_ref, slope_ref):
        scores = scores * scale
        silu, slope = silu_and_slope(scores)
        probs = (silu * w).astype(jnp.bfloat16)
        probs_ref[...] = probs
        slope_ref[...] = slope * w
        return probs

    down, across = iotas(rows)
    w = weight(me * rows + down, me * rows + across)

    def near_forward(h, at):
        probs = pointwise(dot_nt(near(Q, at), near(K, at)), w, row_probs.at[h], row_slope.at[h])
        attended[:, at] = dot_nn(probs, near(V, at))

    each_head(4, near_forward)

    near_w = weight(me * rows + across, me * rows + down)

    def near_column(h, at):
        pointwise(dot_nt(near(K, at), near(Q, at)), near_w, col_probs.at[h], col_slope.at[h])

    each_head(4, near_column)

    arrive_all(K)
    for g in range(groups):
        first = 1 + g * wide

        @pl.when(me >= first)
        def _():
            if not relayed:
                arrive_group(K, first)
            down, across = iotas(wide * rows)
            s = (me - first) * rows + across - jnp.where(across >= rows, 2 * rows, 0)
            w = weight(me * rows + down, s)

            def body(h, at):
                scores = dot_nt(near(Q, at), far(K, first, at))
                pointwise(scores, w, far_row_probs.at[g, h], far_row_slope.at[g, h])

            each_head(4, body)

    arrive_all(V)
    if relayed:
        @pl.when(me == 3)
        def _():
            for c in everything[PIECES // 2 :]:
                send(Q, 1, c).start()
    for g in range(groups):
        first = 1 + g * wide

        @pl.when(me >= first)
        def _():
            if not relayed:
                arrive_group(V, first)

            def body(h, at):
                attended[:, at] += dot_nn(far_row_probs[g, h], far(V, first, at))

            each_head(4, body)

    for copy in loads[3:5]:
        copy.wait()
    gain = gain_ref[...]
    step = piece

    @pl.loop(0, HALVES)
    def _(half):
        pieces = [half * (PIECES // HALVES) + c for c in range(PIECES // HALVES)]
        for c in pieces:
            at = span(c)
            att = attended[at, :]
            center = att - jnp.mean(att, axis=1, keepdims=True)
            rstd = lax.rsqrt(jnp.mean(center * center, axis=1, keepdims=True) + 1e-05)
            normed = center * rstd
            dnorm = grad[at, :].astype(jnp.float32) * gate[at, :].astype(jnp.float32) * gain
            back = rstd * (
                dnorm
                - jnp.mean(dnorm, axis=1, keepdims=True)
                - normed * jnp.mean(dnorm * normed, axis=1, keepdims=True)
            )
            attended[at, :] = normed
            blocks[G, 0, at, :] = back.astype(jnp.bfloat16)
        start(G, pieces)

    part[...] = jnp.zeros((1, width), jnp.float32)

    @pl.loop(0, rows // step)
    def _(i):
        at = pl.ds(pl.multiple_of(i * step, step), step)
        normed = attended[at, :]
        gate_f = gate[at, :].astype(jnp.float32)
        grad_f = grad[at, :].astype(jnp.float32)
        results[0, at, :] = (normed * gain * gate_f).astype(jnp.bfloat16)
        results[1, at, :] = (grad_f * normed * gain).astype(jnp.bfloat16)
        part[...] += jnp.sum(grad_f * gate_f * normed, axis=0, keepdims=True)

    def seq_share(j):
        return pltpu.make_async_remote_copy(
            src_ref=part, dst_ref=seq_parts.at[me],
            send_sem=seq_send.at[j], recv_sem=seq_recv.at[me],
            device_id={"seq": lax.rem(me + j, n)}, device_id_type=MESH,
        )

    def own_share(j):
        return pltpu.make_async_remote_copy(
            src_ref=total, dst_ref=own_parts.at[mine],
            send_sem=own_send.at[j], recv_sem=own_recv.at[mine],
            device_id={"own": lax.rem(mine + j, m)}, device_id_type=MESH,
        )

    pl.loop(1, n)(lambda j: seq_share(j).start())
    seq_parts[me] = part[...]

    def store(i, dst):
        return pltpu.make_async_copy(results.at[i], dst.at[0], store_sem.at[i])

    stores = [store(i, dst) for i, dst in enumerate((out_hbm, gg_hbm, gq_hbm, gk_hbm, gv_hbm))]
    stores[0].start()
    stores[1].start()

    def near_back(h, at):
        grad_probs = dot_nt(near(G, at), near(V, at))
        gq_sum[:, at] = dot_nn((grad_probs * row_slope[h]).astype(jnp.bfloat16), near(K, at))
        grad_probs = dot_nt(near(V, at), near(G, at))
        gk_sum[:, at] = dot_nn((grad_probs * col_slope[h]).astype(jnp.bfloat16), near(Q, at))
        gv_sum[:, at] = dot_nn(col_probs[h], near(G, at))

    each_head(4, near_back)
    for g in range(groups):
        first = 1 + g * wide

        @pl.when(me >= first)
        def _():
            def body(h, at):
                grad_probs = dot_nt(near(G, at), far(V, first, at))
                grad_scores = (grad_probs * far_row_slope[g, h]).astype(jnp.bfloat16)
                gq_sum[:, at] += dot_nn(grad_scores, far(K, first, at))

            each_head(4, body)

    results[2] = (gq_sum[...] * scale).astype(jnp.bfloat16)
    stores[2].start()

    def columns(first, body):
        if wide == 2:
            pl.when(me + first + 1 < n)(functools.partial(body, 2))
            pl.when(me + first + 1 == n)(functools.partial(body, 1))
        else:
            pl.when(me + first < n)(functools.partial(body, 1))

    def far_column(g, first, slots):
        count = slots * rows // HALVES
        down, across = iotas(count)
        lanes = pl.ds(0, count)
        for half in range(HALVES):
            t = (me + first) * rows + half * (rows // HALVES) + across
            if slots == 2:
                t = t + jnp.where(across >= rows // HALVES, rows - rows // HALVES, 0)
            w = weight(t, me * rows + down)

            def body(h, at):
                scores = dot_nt(near(K, at), far_half(Q, first, slots, half, at))
                pointwise(scores, w, far_col_probs.at[g, half, h, :, lanes], far_col_slope.at[g, half, h, :, lanes])

            each_head(4, body)

    def far_column_back(g, first, half, slots):
        lanes = pl.ds(0, slots * rows // HALVES)

        def body(h, at):
            back = far_half(G, first, slots, half, at)
            grad_probs = dot_nt(near(V, at), back)
            grad_scores = (grad_probs * far_col_slope[g, half, h, :, lanes]).astype(jnp.bfloat16)
            key_sum = gk_sum[:, at] + dot_nn(grad_scores, far_half(Q, first, slots, half, at))
            value_sum = gv_sum[:, at] + dot_nn(far_col_probs[g, half, h, :, lanes], back)
            if groups == 1 and half == HALVES - 1:
                results[3, :, at] = (key_sum * scale).astype(jnp.bfloat16)
                results[4, :, at] = value_sum.astype(jnp.bfloat16)
            else:
                gk_sum[:, at] = key_sum
                gv_sum[:, at] = value_sum

        each_head(4, body)

    def sum_over_seq():
        @pl.loop(1, n)
        def _(j):
            src = lax.rem(me + j, n)
            pltpu.make_async_remote_copy(
                src_ref=part, dst_ref=seq_parts.at[src],
                send_sem=seq_send.at[j], recv_sem=seq_recv.at[src],
                device_id={"seq": src}, device_id_type=MESH,
            ).wait_recv()

        group = seq_parts[0]
        for j in range(1, n):
            group = group + seq_parts[j]
        total[...] = group
        pl.loop(1, m)(lambda j: own_share(j).start())
        own_parts[mine] = group

    arrive_all(Q)
    for g in range(groups):
        first = 1 + g * wide
        if not relayed:
            arrive_group(Q, first)
        columns(first, functools.partial(far_column, g, first))

    for half in range(HALVES):
        pieces = everything[half * PIECES // HALVES : (half + 1) * PIECES // HALVES]
        arrive_all(G, pieces)
        if half == 0:
            sum_over_seq()
        for g in range(groups):
            first = 1 + g * wide
            if not relayed:
                arrive_group(G, first, pieces)
            columns(first, functools.partial(far_column_back, g, first, half))

    @pl.when((me == n - 1) | (groups > 1))
    def _():
        results[3] = (gk_sum[...] * scale).astype(jnp.bfloat16)
        results[4] = gv_sum[...].astype(jnp.bfloat16)

    stores[3].start()
    stores[4].start()

    @pl.loop(1, m)
    def _(j):
        src = lax.rem(mine + j, m)
        pltpu.make_async_remote_copy(
            src_ref=total, dst_ref=own_parts.at[src],
            send_sem=own_send.at[j], recv_sem=own_recv.at[src],
            device_id={"own": src}, device_id_type=MESH,
        ).wait_recv()

    whole = own_parts[0]
    for j in range(1, m):
        whole = whole + own_parts[j]
    part_sum[...] = whole
    last = pltpu.make_async_copy(part_sum, ggain_hbm, store_sem.at[5])
    last.start()

    for what in (K, V, Q, G):
        wait_sends(what)
        if relayed:
            @pl.when(me == (3 if later(what) else 0))
            def _():
                for c in everything:
                    relay(what, c).wait_send()
    pl.loop(1, n)(lambda j: seq_share(j).wait_send())
    pl.loop(1, m)(lambda j: own_share(j).wait_send())
    for copy in stores + [last]:
        copy.wait()


def finish(*refs):
    sources, results, held, sem = refs[:6], refs[6:12], refs[12:18], refs[18]
    loads = [pltpu.make_async_copy(a, b, sem.at[0, i]) for i, (a, b) in enumerate(zip(sources, held))]
    stores = [pltpu.make_async_copy(a, b, sem.at[1, i]) for i, (a, b) in enumerate(zip(held, results))]
    for copy in loads:
        copy.start()
    for load, store in zip(loads, stores):
        load.wait()
        store.start()
    for copy in stores:
        copy.wait()


def per_device(n, m, queries, keys, values, gates, lengths, gain, grad_out):
    rows, width = queries.shape[1], queries.shape[2]
    head = width // H
    reach = min(n - 1, (rows * n // 2 - 1) // rows + 1)
    slots = reach + 1
    wide = 2 if reach % 2 == 0 else 1
    groups = reach // wide
    hbm = pl.BlockSpec(memory_space=pltpu.HBM)
    any_spec = pl.BlockSpec(memory_space=pl.ANY)
    block = jax.ShapeDtypeStruct(queries.shape, jnp.bfloat16)
    shapes = [block] * 5 + [jax.ShapeDtypeStruct((1, width), jnp.float32)]
    dma = pltpu.SemaphoreType.DMA
    outs = pl.pallas_call(
        functools.partial(kernel, n, m, reach, wide, 1.0 / math.sqrt(head)),
        out_shape=shapes,
        in_specs=[hbm] * 7,
        out_specs=[any_spec] * 6,
        scratch_shapes=[
            pltpu.SMEM(lengths.shape, jnp.int32),
            pltpu.VMEM((1, width), jnp.float32),
            pltpu.VMEM((4, slots, rows, width), jnp.bfloat16),
            pltpu.VMEM((rows, width), jnp.bfloat16),
            pltpu.VMEM((rows, width), jnp.bfloat16),
            pltpu.VMEM((H, rows, rows), jnp.bfloat16),
            pltpu.VMEM((H, rows, rows), jnp.float32),
            pltpu.VMEM((H, rows, rows), jnp.bfloat16),
            pltpu.VMEM((H, rows, rows), jnp.float32),
            pltpu.VMEM((groups, H, rows, wide * rows), jnp.bfloat16),
            pltpu.VMEM((groups, H, rows, wide * rows), jnp.float32),
            pltpu.VMEM((groups, HALVES, H, rows, wide * rows // HALVES), jnp.bfloat16),
            pltpu.VMEM((groups, HALVES, H, rows, wide * rows // HALVES), jnp.float32),
            pltpu.VMEM((rows, width), jnp.float32),
            pltpu.VMEM((rows, width), jnp.float32),
            pltpu.VMEM((rows, width), jnp.float32),
            pltpu.VMEM((rows, width), jnp.float32),
            pltpu.VMEM((5, rows, width), jnp.bfloat16),
            pltpu.VMEM((1, width), jnp.float32),
            pltpu.VMEM((n, 1, width), jnp.float32),
            pltpu.VMEM((1, width), jnp.float32),
            pltpu.VMEM((m, 1, width), jnp.float32),
            pltpu.VMEM((1, width), jnp.float32),
            dma((7,)), dma((6,)), dma((4, slots, PIECES)), dma((4, slots, PIECES)), dma((4, PIECES)),
            dma((n,)), dma((n,)), dma((m,)), dma((m,)),
        ],
        compiler_params=pltpu.CompilerParams(
            collective_id=0, has_side_effects=True, vmem_limit_bytes=ROOM
        ),
        cost_estimate=pl.CostEstimate(
            flops=16 * slots * rows * rows * width, bytes_accessed=20 * rows * width, transcendentals=0
        ),
    )(lengths, gain.reshape(1, width), queries, keys, values, gates, grad_out)
    output, grad_q, grad_k, grad_v, grad_gate, grad_gain = pl.pallas_call(
        finish,
        out_shape=shapes,
        in_specs=[any_spec] * 6,
        out_specs=[any_spec] * 6,
        scratch_shapes=[pltpu.VMEM(x.shape, x.dtype) for x in shapes] + [dma((2, 6))],
        compiler_params=pltpu.CompilerParams(has_side_effects=True, vmem_limit_bytes=ROOM),
    )(*outs)
    return output, grad_q, grad_k, grad_v, grad_gate, grad_gain.reshape(width)


def solution(mesh):
    blocked = P("own", "seq", None)
    sizes = (mesh.shape["seq"], mesh.shape["own"])
    return jax.shard_map(
        functools.partial(per_device, *sizes),
        mesh=mesh,
        in_specs=(blocked, blocked, blocked, blocked, P("own", None), P(), blocked),
        out_specs=(blocked, blocked, blocked, blocked, blocked, P()),
        check_vma=False,
    )
```
